128 devices in a mesh: fsdp: 32 (over y, z, core), rep: 4 (over x).
Axes of the slice: x: 4, y: 4, z: 4, core: 2. Of those that a mesh axis runs over, the one named last changes fastest.
Arguments:
- grad_partial: bfloat16 [4, 32, 1024, 1024], P('rep', None, 'fsdp'), may hold values from -52 to 52
- second_moment: float32 [32, 1024, 1024], P(None, 'fsdp', 'rep'), may hold values from 0.02 to 150
- left_factor: bfloat16 [96, 1024, 1024], P('fsdp'), may hold values from -0.6 to 2.6
- right_factor: bfloat16 [96, 1024, 1024], P('fsdp'), may hold values from -0.6 to 2.6
- block_owner: int32 [32], replicated, may hold values from 0 to 31, as said below
- block_slot: int32 [32], replicated, may hold values from 0 to 2, as said below
Outputs:
- update: bfloat16 [32, 1024, 1024], P(None, 'fsdp', 'rep')
- new_moment: float32 [32, 1024, 1024], P(None, 'fsdp', 'rep')
The draws below stay inside these ranges and needn't reach their ends.
Inputs may be any that keep to these rules, and one draw needn't show every extreme that they name: `block_owner`: each device owns at most 3 blocks, and some device owns exactly 3. `block_slot`: no two blocks share an owner and a slot; a device that owns c blocks holds them at slots 0 to c - 1; the factors of the block at owner d, slot s are entry d * 3 + s of left_factor and right_factor.
All inputs are finite; a program needn't handle non-finite values.
Results may differ from the reference program's by a relative error of at most 0.017.
Values may be sent and summed in bfloat16 or wider, within the bound.
A program may use at most 128 MiB of HBM per device.

```python
import math
import jax
import jax.numpy as jnp
from jax import lax

BLOCK_ORDER = 1024
CAP = 3
NBLK = 32
FACTOR_SLOTS = 96
N_FSDP = 32
N_REP = 4


def routing(key):
    groups = N_FSDP // 4
    key_pick, key_order, key_force, key_perm = jax.random.split(key, 4)
    table = jnp.array([[3, 1, 0, 0], [2, 1, 1, 0], [1, 1, 1, 1], [2, 2, 0, 0]], jnp.int32)
    pick = jax.random.randint(key_pick, (groups,), 0, 4)
    forced = jax.random.randint(key_force, (), 0, groups)
    pick = jnp.where(jnp.arange(groups) == forced, 0, pick)
    patterns = table[pick]
    scores = jax.random.randint(key_order, (groups, 4), 0, 1 << 20) * 4 + jnp.arange(4, dtype=jnp.int32)[None, :]
    order = jnp.argsort(scores, axis=1)
    counts = jnp.take_along_axis(patterns, order, axis=1).reshape(N_FSDP)
    ends = jnp.cumsum(counts)
    starts = ends - counts
    position = jnp.arange(NBLK, dtype=jnp.int32)
    owner_sorted = jnp.sum(position[:, None] >= ends[None, :], axis=1).astype(jnp.int32)
    slot_sorted = position - starts[owner_sorted]
    permuted = jax.random.permutation(key_perm, NBLK)
    return (owner_sorted[permuted].astype(jnp.int32), slot_sorted[permuted].astype(jnp.int32))


def draw_block_owner(key, part):
    return routing(key)[0]


def draw_block_slot(key, part):
    return routing(key)[1]


def factor_matrix(key, spread_amount):
    key_diagonal, key_offdiagonal = jax.random.split(key)
    diagonal_part = jnp.exp(jax.random.uniform(key_diagonal, (FACTOR_SLOTS, BLOCK_ORDER), jnp.float32, math.log(0.5), math.log(2.0)))
    offdiagonal_part = jnp.clip(jax.random.normal(key_offdiagonal, (FACTOR_SLOTS, BLOCK_ORDER, BLOCK_ORDER), jnp.float32), -6.0, 6.0) * (spread_amount / math.sqrt(BLOCK_ORDER))
    identity = (jnp.arange(BLOCK_ORDER)[:, None] == jnp.arange(BLOCK_ORDER)[None, :]).astype(jnp.float32)
    return (offdiagonal_part * (1.0 - identity) + diagonal_part[:, :, None] * identity).astype(jnp.bfloat16)


def draw_left_factor(key, part):
    key = jax.random.fold_in(key, 11)
    return factor_matrix(key, 0.5)


def draw_right_factor(key, part):
    key = jax.random.fold_in(key, 12)
    return factor_matrix(key, 0.5)


def draw_second_moment(key, part):
    key = jax.random.fold_in(key, 7)
    key_level, key_sign, key_row, key_col, key_entry = jax.random.split(key, 5)
    shape = (NBLK, BLOCK_ORDER, BLOCK_ORDER)
    position = (jnp.arange(BLOCK_ORDER, dtype=jnp.float32) + 0.5) / BLOCK_ORDER - 0.5
    direction = jnp.where(jax.random.permutation(key_sign, NBLK) % 2 == 0, 1.0, -1.0).astype(jnp.float32)[:, None, None]
    row_profile = jnp.exp(math.log(10.0) * direction * position[None, :, None])
    row_rough = jnp.exp(jax.random.uniform(key_row, (NBLK, BLOCK_ORDER, 1), jnp.float32, 0.0, math.log(1.5)))
    col_scale = jnp.exp(jax.random.uniform(key_col, (NBLK, 1, BLOCK_ORDER), jnp.float32, -0.5 * math.log(10.0), 0.5 * math.log(10.0)))
    level = jnp.exp(jax.random.uniform(key_level, (NBLK, 1, 1), jnp.float32, math.log(0.2), math.log(5.0)))
    entry = jnp.exp(jax.random.uniform(key_entry, shape, jnp.float32, 0.0, math.log(2.0)))
    return level * row_profile * row_rough * col_scale * entry


def draw_grad_partial(key, part):
    key = jax.random.fold_in(key, 5)
    key_rough, key_cols, key_base = jax.random.split(key, 3)
    shape = (N_REP, NBLK, BLOCK_ORDER, BLOCK_ORDER)
    rising = jnp.exp(math.log(10.0) * jnp.arange(BLOCK_ORDER, dtype=jnp.float32) / BLOCK_ORDER)
    rough = jnp.exp(jax.random.uniform(key_rough, (NBLK, BLOCK_ORDER, 1), jnp.float32, 0.0, math.log(2.0)))
    row_scale = rough * rising[None, :, None]
    col_scale = jnp.exp(jax.random.uniform(key_cols, (NBLK, 1, BLOCK_ORDER), jnp.float32, 0.0, math.log(10.0)))
    rep_scale = (1.0 + 2.0 * jnp.arange(N_REP, dtype=jnp.float32) / max(N_REP - 1, 1))[:, None, None, None]
    noise = jnp.clip(jax.random.normal(key_base, shape, jnp.float32), -6.0, 6.0) * rep_scale
    return (noise * row_scale[None] * col_scale[None] / 100.0).astype(jnp.bfloat16)


def setup_inputs(seed: int = 0) -> dict:
    arg_keys = jax.random.split(jax.random.key(seed), 7)
    grad_partial = draw_grad_partial(jax.random.fold_in(arg_keys[6], 71), 0)
    second_moment = draw_second_moment(jax.random.fold_in(arg_keys[6], 71), 0)
    left_factor = draw_left_factor(jax.random.fold_in(arg_keys[6], 71), 0)
    right_factor = draw_right_factor(jax.random.fold_in(arg_keys[6], 71), 0)
    block_owner = draw_block_owner(jax.random.fold_in(arg_keys[6], 71), 0)
    block_slot = draw_block_slot(jax.random.fold_in(arg_keys[6], 71), 0)
    return {"grad_partial": grad_partial, "second_moment": second_moment, "left_factor": left_factor, "right_factor": right_factor, "block_owner": block_owner, "block_slot": block_slot}


def reference(grad_partial, second_moment, left_factor, right_factor, block_owner, block_slot):
    summed = lax.optimization_barrier(jnp.sum(grad_partial.astype(jnp.float32), axis=0))
    new_moment = 0.99 * second_moment + 0.01 * summed * summed
    adam = summed / (jnp.sqrt(new_moment) + 1e-08)
    adam_rms = jnp.sqrt(lax.optimization_barrier(jnp.mean(adam * adam, axis=(1, 2))))
    factor_index = (block_owner * CAP + block_slot).astype(jnp.int32)

    def precondition(inputs):
        grad_block, which, rms_value = inputs
        left_prod = jnp.dot(left_factor[which], grad_block.astype(jnp.bfloat16), preferred_element_type=jnp.float32).astype(jnp.bfloat16)
        product = jnp.dot(left_prod, right_factor[which], preferred_element_type=jnp.float32)
        graft = rms_value / jnp.sqrt(jnp.mean(product * product) + 1e-06)
        return (product * graft).astype(jnp.bfloat16)
    update = lax.map(precondition, (summed, factor_index, adam_rms))
    return (update, new_moment)
```

```python
import functools

import jax
import jax.numpy as jnp
from jax import lax
from jax.experimental import pallas as pl
from jax.experimental.pallas import tpu as pltpu
from jax.sharding import PartitionSpec as P

MESH = pl.DeviceIdType.MESH
REPS = 4
CHIPS = 16
SIDE = 4
PER_PLANE = 8
HALF = PER_PLANE // 2
ORDER_AT = 0
DEST_AT = 32
SLOT_AT = 96
CORE_AT = 97
PLACE_AT = 128
FROM_AT = 160
TABLE = 192


def step_kernel(
    tab, g_hbm, sm_hbm, l_hbm, r_hbm, upd_hbm, nm_hbm,
    grad, sm, left, right, xs, a_in, b_in, c_in, c_out, summed, f_out, g_in,
    lp, prod, pb0, pb1, pb2, pb3, ret, back, mom_in, nm, upd,
    ad_x, ad_1, ad_p, ad_2, ad_3, rms,
    sem_in, sem_out, x_send, x_recv, f_send, f_recv, d_send, d_recv,
    p_send, p_recv, u_send, u_recv, m_send, m_recv, s_send, s_recv,
):
    pbs = (pb0, pb1, pb2, pb3)
    f = lax.axis_index("fsdp")
    x = lax.axis_index("rep")
    core = f % 2
    chip = f // 2
    cy = chip // SIDE
    cz = chip % SIDE
    sibling = f + 1 - 2 * core
    nblk, rows, width = grad.shape
    quarter = width // REPS

    def chip_at(i):
        return ((cy + i // SIDE) % SIDE) * SIDE + (cz + i % SIDE) % SIDE

    loads = [
        pltpu.make_async_copy(src, dst, sem_in.at[i])
        for i, (src, dst) in enumerate(
            ((g_hbm, grad), (l_hbm, left), (r_hbm, right), (sm_hbm, sm))
        )
    ]
    for load in loads:
        load.start()

    barrier = pltpu.get_barrier_semaphore()

    def greet(i, _):
        to = (chip_at(i // REPS) * 2 + core, (x + i % REPS) % REPS)
        pl.semaphore_signal(barrier, inc=1, device_id=to, device_id_type=MESH)
        return 0

    lax.fori_loop(1, CHIPS * REPS, greet, 0)
    pl.semaphore_signal(barrier, inc=1, device_id=(sibling, x), device_id_type=MESH)

    slot = tab[SLOT_AT]
    holder = tab[CORE_AT]
    x_right, x_left, x_far = (x + 1) % REPS, (x + 3) % REPS, (x + 2) % REPS

    def stage(k):
        def body(t, _):
            xs[k, t] = grad[tab[ORDER_AT + t], :, k * quarter : (k + 1) * quarter]
            return 0

        lax.fori_loop(0, nblk, body, 0, unroll=4)

    def x_copy(k, n, src, dst, to):
        i = k * 6 + n
        return pltpu.make_async_remote_copy(
            src, dst, x_send.at[i], x_recv.at[i], device_id=(f, to), device_id_type=MESH
        )

    def x_copies(k):
        far, near_r, near_l = x_far * PER_PLANE, x_right * PER_PLANE, x_left * PER_PLANE
        return (
            x_copy(k, 0, xs.at[k, pl.ds(far, HALF)], a_in.at[0, k], x_right),
            x_copy(k, 1, xs.at[k, pl.ds(far + HALF, HALF)], a_in.at[1, k], x_left),
            x_copy(k, 2, xs.at[k, pl.ds(near_r + HALF, HALF)], b_in.at[0, k], x_right),
            x_copy(k, 3, xs.at[k, pl.ds(near_l, HALF)], b_in.at[1, k], x_left),
            x_copy(k, 4, c_out.at[0, k], c_in.at[0, k], x_right),
            x_copy(k, 5, c_out.at[1, k], c_in.at[1, k], x_left),
        )

    xc = [x_copies(k) for k in range(REPS)]

    def first(k):
        for n in range(4):
            xc[k][n].start()

    def wide(v):
        return v.astype(jnp.float32)

    def merge(k):
        for side, at in ((0, x_right * PER_PLANE), (1, x_left * PER_PLANE + HALF)):
            xc[k][side].wait_recv()

            def body(j, _):
                c_out[side, k, j] = (wide(xs[k, at + j]) + wide(a_in[side, k, j])).astype(jnp.bfloat16)
                return 0

            lax.fori_loop(0, HALF, body, 0, unroll=True)
            xc[k][4 + side].start()

    def finish(k):
        for n in (2, 3, 4, 5):
            xc[k][n].wait_recv()
        for lo, from_l, from_r in ((0, c_in, b_in), (HALF, b_in, c_in)):

            def body(j, _):
                total = wide(xs[k, x * PER_PLANE + lo + j]) + wide(from_l[0, k, j]) + wide(from_r[1, k, j])
                summed[k, lo + j] = total.astype(jnp.bfloat16)
                return 0

            lax.fori_loop(0, HALF, body, 0, unroll=True)

    def forward(k):
        def body(i, _):
            to = chip_at(i)
            f_out[k, to] = summed[k, tab[DEST_AT + x * CHIPS + to]]
            pltpu.make_async_remote_copy(
                f_out.at[k, to], g_in.at[k, chip, core], f_send.at[k], f_recv.at[k],
                device_id=(to * 2 + core, x), device_id_type=MESH,
            ).start()
            return 0

        lax.fori_loop(1, CHIPS, body, 0)
        g_in[k, chip, core] = summed[k, tab[DEST_AT + x * CHIPS + chip]]

    def many(ref, send, recv):
        return pltpu.make_async_remote_copy(
            ref, ref, send, recv, device_id=(sibling, x), device_id_type=MESH
        )

    swaps = [
        pltpu.make_async_remote_copy(
            g_in.at[k, :, core], g_in.at[k, :, core], d_send.at[k], d_recv.at[k],
            device_id=(sibling, x), device_id_type=MESH,
        )
        for k in range(REPS)
    ]

    def swap(k):
        many(f_out.at[k, pl.ds(0, CHIPS - 1)], f_send.at[k], f_recv.at[k]).wait_recv()
        swaps[k].start()

    tile = width // 2

    def left_mul(k):
        swaps[k].wait_recv()

        def body(i, _):
            at = pl.multiple_of(i * tile, tile)
            part = jnp.dot(
                left[slot, pl.ds(at, tile), :], g_in[k].reshape(width, quarter),
                preferred_element_type=jnp.float32,
            )
            lp[pl.ds(at, tile), k * quarter : (k + 1) * quarter] = part.astype(jnp.bfloat16)
            return 0

        lax.fori_loop(0, width // tile, body, 0)

    loads[0].wait()
    stage(0)
    pl.semaphore_wait(barrier, CHIPS * REPS)
    first(0)
    stage(1)
    first(1)
    merge(0)
    stage(2)
    first(2)
    merge(1)
    finish(0)
    forward(0)
    stage(3)
    first(3)
    merge(2)
    finish(1)
    forward(1)
    loads[1].wait()
    swap(0)
    merge(3)
    left_mul(0)
    finish(2)
    forward(2)
    swap(1)
    left_mul(1)
    finish(3)
    forward(3)

    moments = []
    for i in range(1, REPS):
        to = (x + i) % REPS
        moments.append(
            pltpu.make_async_remote_copy(
                summed.at[to], mom_in.at[x], m_send.at[i], m_recv.at[i],
                device_id=(f, to), device_id_type=MESH,
            )
        )
        moments[-1].start()
    mom_in[x] = summed[x]

    swap(2)
    left_mul(2)

    loads[3].wait()
    for copy in moments:
        copy.wait_recv()

    def moment(b, _):
        t = tab[PLACE_AT + b]
        s = wide(mom_in[t // PER_PLANE, t % PER_PLANE])
        new = 0.99 * sm[b] + 0.01 * s * s
        nm[b] = new
        adam = s / (jnp.sqrt(new) + 1e-08)
        sq = jnp.sum(adam * adam, axis=0, keepdims=True)
        half = quarter // 2
        ad_x[x, pl.ds(b, 1), :] = sq[:, :half] + sq[:, half:]
        return 0

    lax.fori_loop(0, nblk, moment, 0, unroll=2)
    store_nm = pltpu.make_async_copy(nm, nm_hbm, sem_out.at[0])
    store_nm.start()

    sums_x = [
        pltpu.make_async_remote_copy(
            ad_x.at[x], ad_x.at[x], s_send.at[i], s_recv.at[i],
            device_id=(f, (x + i) % REPS), device_id_type=MESH,
        )
        for i in range(1, REPS)
    ]
    for copy in sums_x:
        copy.start()

    swap(3)
    left_mul(3)

    for copy in sums_x:
        copy.wait_recv()
    ad_1[...] = (ad_x[0] + ad_x[1]) + (ad_x[2] + ad_x[3])

    def sums_plane(i, _):
        to = chip_at(i)
        pltpu.make_async_remote_copy(
            ad_1, ad_p.at[chip], s_send.at[0], s_recv.at[0],
            device_id=(to * 2 + core, x), device_id_type=MESH,
        ).start()
        return 0

    lax.fori_loop(1, CHIPS, sums_plane, 0)
    ad_p[chip] = ad_1[...]

    loads[2].wait()
    squares = jnp.zeros((1, quarter), jnp.float32)
    for i in range(REPS):
        q = (x + i) % REPS
        cols = pl.ds(pl.multiple_of(q * quarter, quarter), quarter)

        def body(n, acc):
            at = pl.multiple_of(n * tile, tile)
            part = jnp.dot(
                lp[pl.ds(at, tile), :], right[slot, :, cols], preferred_element_type=jnp.float32
            )
            prod[i, pl.ds(at, tile), :] = part
            return acc + jnp.sum(part * part, axis=0, keepdims=True)

        squares = lax.fori_loop(0, width // tile, body, squares)

    many(ad_p.at[pl.ds(0, CHIPS - 1)], s_send.at[0], s_recv.at[0]).wait_recv()
    ad_2[...] = jnp.sum(ad_p[...], axis=0)
    sums_chip = pltpu.make_async_remote_copy(
        ad_2, ad_3, s_send.at[REPS], s_recv.at[REPS], device_id=(sibling, x), device_id_type=MESH
    )
    sums_chip.start()

    mean = jnp.sum(squares, axis=1, keepdims=True) / (width * width)
    inverse = 1.0 / jnp.sqrt(mean + 1e-06)
    trades = []
    for i in range(REPS):
        pb = pbs[i]

        def body(n, _):
            at = pl.multiple_of(n * 2 * rows, 2 * rows)
            scaled = (prod[i, pl.ds(at, 2 * rows), :] * inverse).astype(jnp.bfloat16)
            pb[core, n] = scaled.reshape(2, rows, quarter)
            return 0

        lax.fori_loop(0, CHIPS, body, 0, unroll=2)
        trades.append(
            pltpu.make_async_remote_copy(
                pb.at[core, :, 1 - core], pb.at[core, :, 1 - core], p_send.at[i], p_recv.at[i],
                device_id=(sibling, x), device_id_type=MESH,
            )
        )
        trades[i].start()

    for i in range(REPS):
        pb = pbs[i]
        q = (x + i) % REPS
        trades[i].wait_recv()

        def body(n, _):
            to = chip_at(n)
            ret[i, to] = pb[holder, to, core]
            pltpu.make_async_remote_copy(
                ret.at[i, to], back.at[x * CHIPS + chip], u_send.at[0], u_recv.at[0],
                device_id=(to * 2 + core, q), device_id_type=MESH,
            ).start()
            return 0

        lax.fori_loop(1 if i == 0 else 0, CHIPS, body, 0)
        if i == 0:
            back[x * CHIPS + chip] = pb[holder, chip, core]

    sums_chip.wait_recv()
    total = jnp.sum(ad_2[...] + ad_3[...], axis=1, keepdims=True)
    rms[...] = jnp.broadcast_to(jnp.sqrt(total / (width * width)), rms.shape)

    many(back.at[pl.ds(0, CHIPS * REPS - 1)], u_send.at[0], u_recv.at[0]).wait_recv()

    def collect(b, _):
        scale = rms[pl.ds(b, 1), :]
        scale = jnp.concatenate([scale, scale], axis=1)
        upd[b] = (wide(back[tab[FROM_AT + b]]) * scale).astype(jnp.bfloat16)
        return 0

    lax.fori_loop(0, nblk, collect, 0, unroll=2)
    store_upd = pltpu.make_async_copy(upd, upd_hbm, sem_out.at[1])
    store_upd.start()

    for k in range(REPS):
        for copy in xc[k]:
            copy.wait_send()
        many(f_out.at[k, pl.ds(0, CHIPS - 1)], f_send.at[k], f_recv.at[k]).wait_send()
        swaps[k].wait_send()
        trades[k].wait_send()
    for copy in moments + sums_x + [sums_chip]:
        copy.wait_send()
    many(ad_p.at[pl.ds(0, CHIPS - 1)], s_send.at[0], s_recv.at[0]).wait_send()
    many(back.at[pl.ds(0, CHIPS * REPS - 1)], u_send.at[0], u_recv.at[0]).wait_send()
    store_nm.wait()
    store_upd.wait()


def one_kernel(grad, second_moment, left_factor, right_factor, table):
    nblk, rows, width = grad.shape
    slots = left_factor.shape[0]
    quarter = width // REPS
    bf, f32 = jnp.bfloat16, jnp.float32
    piece = (rows, quarter)
    any_spec = pl.BlockSpec(memory_space=pl.ANY)
    vmem = pltpu.VMEM
    dma = pltpu.SemaphoreType.DMA
    return pl.pallas_call(
        step_kernel,
        out_shape=(
            jax.ShapeDtypeStruct((nblk, rows, quarter), bf),
            jax.ShapeDtypeStruct((nblk, rows, quarter), f32),
        ),
        in_specs=[pl.BlockSpec(memory_space=pltpu.SMEM)] + [any_spec] * 4,
        out_specs=(any_spec, any_spec),
        scratch_shapes=[
            vmem((nblk, rows, width), bf),
            vmem((nblk, rows, quarter), f32),
            vmem((slots, width, width), bf),
            vmem((slots, width, width), bf),
            vmem((REPS, nblk) + piece, bf),
            vmem((2, REPS, HALF) + piece, bf),
            vmem((2, REPS, HALF) + piece, bf),
            vmem((2, REPS, HALF) + piece, bf),
            vmem((2, REPS, HALF) + piece, bf),
            vmem((REPS, PER_PLANE) + piece, bf),
            vmem((REPS, CHIPS) + piece, bf),
            vmem((REPS, CHIPS, 2) + piece, bf),
            vmem((width, width), bf),
            vmem((REPS, width, quarter), f32),
        ]
        + [vmem((2, CHIPS, 2) + piece, bf)] * REPS
        + [
            vmem((REPS, CHIPS) + piece, bf),
            vmem((REPS * CHIPS,) + piece, bf),
            vmem((REPS, PER_PLANE) + piece, bf),
            vmem((nblk,) + piece, f32),
            vmem((nblk,) + piece, bf),
            vmem((REPS, nblk, 128), f32),
            vmem((nblk, 128), f32),
            vmem((CHIPS, nblk, 128), f32),
            vmem((nblk, 128), f32),
            vmem((nblk, 128), f32),
            vmem((nblk, 128), f32),
            dma((4,)),
            dma((2,)),
            dma((REPS * 6,)),
            dma((REPS * 6,)),
        ]
        + [dma((REPS,))] * 6
        + [dma((1,)), dma((1,)), dma((REPS,)), dma((REPS,)), dma((REPS + 1,)), dma((REPS + 1,))],
        compiler_params=pltpu.CompilerParams(
            collective_id=0, has_side_effects=True, vmem_limit_bytes=58 << 20
        ),
        cost_estimate=pl.CostEstimate(
            flops=4 * width**3, bytes_accessed=18 << 20, transcendentals=nblk * rows * quarter
        ),
        name="shampoo_step",
    )(table, grad, second_moment, left_factor, right_factor)


def tables(block_owner, block_slot):
    f = lax.axis_index("fsdp")
    x = lax.axis_index("rep")
    nblk = block_owner.shape[0]
    blocks = jnp.arange(nblk, dtype=jnp.int32)

    def pick(values, hit):
        return jnp.sum(jnp.where(hit, values, 0), axis=-1).astype(jnp.int32)

    before = jnp.sum((block_owner[None, :] < block_owner[:, None]).astype(jnp.int32), axis=1)
    place = before + block_slot
    plane = place % REPS
    within = place // REPS
    sorted_at = plane * PER_PLANE + within
    came_from = plane * CHIPS + block_owner // 2
    sites = jnp.arange(REPS * CHIPS, dtype=jnp.int32)
    order = pick(blocks[None, :], sorted_at[None, :] == blocks[:, None])
    dest = pick(within[None, :], came_from[None, :] == sites[:, None])
    slot = pick(block_slot, (block_owner == f) & (plane == x))
    core = pick(block_owner % 2, came_from == x * CHIPS + f // 2)
    pad = jnp.zeros((PLACE_AT - CORE_AT - 1,), jnp.int32)
    table = jnp.concatenate([order, dest, slot[None], core[None], pad, sorted_at, came_from])
    most = jnp.max(jnp.sum(((block_owner // 2)[None, :] == sites[:CHIPS, None]).astype(jnp.int32), axis=1))
    return table, most


def general(grad_partial, second_moment, left_factor, right_factor, block_owner, block_slot):
    slot_count = left_factor.shape[0]
    row_count = grad_partial.shape[2]
    full_width = grad_partial.shape[3]
    rep_count = lax.axis_size("rep")
    owner_count = lax.axis_size("fsdp")
    owner_index = lax.axis_index("fsdp")
    rep_index = lax.axis_index("rep")
    quarter = full_width // rep_count
    slot_range = jnp.arange(slot_count, dtype=jnp.int32)
    owner_range = jnp.arange(owner_count, dtype=jnp.int32)
    selector = (
        (block_slot[None, None, :] == slot_range[:, None, None])
        & (block_owner[None, None, :] == owner_range[None, :, None])
    ).astype(jnp.bfloat16)
    owned = (
        (block_slot[None, :] == slot_range[:, None]) & (block_owner[None, :] == owner_index)
    ).astype(jnp.float32)
    summed = lax.psum(grad_partial[0], "rep").astype(jnp.float32)
    column = lax.dynamic_slice_in_dim(summed, rep_index * quarter, quarter, 2)
    new_moment = 0.99 * second_moment + 0.01 * column * column
    adam = column / (jnp.sqrt(new_moment) + 1e-08)
    partial_squares = jnp.sum(adam * adam, axis=(1, 2))
    total_squares = lax.psum(partial_squares, ("fsdp", "rep"))
    adam_rms = jnp.sqrt(total_squares / (full_width * full_width))
    slot_rms = jnp.sum(owned * adam_rms[None, :], axis=1)
    grad_bf = summed.astype(jnp.bfloat16)
    outbound = jnp.einsum(
        "kdn,nrc->kdrc", selector, grad_bf, preferred_element_type=jnp.float32
    ).astype(jnp.bfloat16)
    outbound = outbound.reshape(slot_count, owner_count * row_count, full_width)
    inbound = lax.all_to_all(outbound, "fsdp", split_axis=1, concat_axis=1, tiled=True)
    left_prod = jnp.einsum(
        "kij,kjc->kic", left_factor, inbound, preferred_element_type=jnp.float32
    ).astype(jnp.bfloat16)
    product = jnp.einsum(
        "kij,kjc->kic", left_prod, right_factor, preferred_element_type=jnp.float32
    )
    prod_mean = jnp.mean(product * product, axis=(1, 2))
    graft = slot_rms / jnp.sqrt(prod_mean + 1e-06)
    scaled = (product * graft[:, None, None]).astype(jnp.bfloat16)
    returned = lax.all_to_all(scaled, "fsdp", split_axis=1, concat_axis=1, tiled=True)
    returned = lax.dynamic_slice_in_dim(returned, rep_index * quarter, quarter, 2)
    returned = returned.reshape(slot_count, owner_count, row_count, quarter)
    update = jnp.einsum(
        "kdn,kdrc->nrc", selector, returned, preferred_element_type=jnp.float32
    ).astype(jnp.bfloat16)
    return (update, new_moment)


def per_device(grad_partial, second_moment, left_factor, right_factor, block_owner, block_slot):
    table, most = tables(block_owner, block_slot)

    def direct(gp, sm, lf, rf, _owner, _slot, tab):
        return one_kernel(gp[0], sm, lf, rf, tab)

    def fallback(gp, sm, lf, rf, owner, slot, _tab):
        return general(gp, sm, lf, rf, owner, slot)

    return lax.cond(
        most <= REPS, direct, fallback,
        grad_partial, second_moment, left_factor, right_factor, block_owner, block_slot, table,
    )


def solution(mesh):
    placed = (
        P("rep", None, "fsdp", None),
        P(None, "fsdp", "rep"),
        P("fsdp", None, None),
        P("fsdp", None, None),
        P(),
        P(),
    )
    return jax.shard_map(
        per_device,
        mesh=mesh,
        in_specs=placed,
        out_specs=(P(None, "fsdp", "rep"), P(None, "fsdp", "rep")),
        check_vma=False,
    )
```

```python
import functools

import jax
import jax.numpy as jnp
from jax import lax
from jax.experimental import pallas as pl
from jax.experimental.pallas import tpu as pltpu
from jax.sharding import PartitionSpec as P

MESH = pl.DeviceIdType.MESH
REPS = 4
CHIPS = 16
SIDE = 4
PER_PLANE = 8
HALF = PER_PLANE // 2


def step_kernel(
    owner, owner_slot, g_hbm, sm_hbm, l_hbm, r_hbm, upd_hbm, nm_hbm,
    grad, sm, left, right, xs, a_in, b_in, c_in, c_out, summed, f_out, g_in,
    lp, pb0, pb1, pb2, pb3, ret, back, mom_in, nm, upd,
    ad_1, ad_2, factor, place_v, place, inverse_v, inverse,
    sem_in, sem_out, x_send, x_recv, f_send, f_recv, d_send, d_recv,
    p_send, p_recv, u_send, u_recv, m_send, m_recv, s_send, s_recv,
):
    pbs = (pb0, pb1, pb2, pb3)
    f = lax.axis_index("fsdp")
    x = lax.axis_index("rep")
    core = f % 2
    chip = f // 2
    cy = chip // SIDE
    cz = chip % SIDE
    sibling = f + 1 - 2 * core
    nblk, rows, width = grad.shape
    quarter = width // REPS

    chips = [
        lax.rem(cy + i // SIDE, SIDE) * SIDE + lax.rem(cz + i % SIDE, SIDE) for i in range(CHIPS)
    ]
    reps = [lax.rem(x + i, REPS) for i in range(REPS)]

    loads = [
        pltpu.make_async_copy(src, dst, sem_in.at[i])
        for i, (src, dst) in enumerate(
            ((g_hbm, grad), (l_hbm, left), (r_hbm, right), (sm_hbm, sm))
        )
    ]
    for load in loads:
        load.start()

    barrier = pltpu.get_barrier_semaphore()

    for i in range(1, CHIPS * REPS):
        to = (chips[i // REPS] * 2 + core, reps[i % REPS])
        pl.semaphore_signal(barrier, inc=1, device_id=to, device_id_type=MESH)
    pl.semaphore_signal(barrier, inc=1, device_id=(sibling, x), device_id_type=MESH)

    lane = lax.broadcasted_iota(jnp.int32, place_v.shape, 1)
    line = lax.broadcasted_iota(jnp.int32, place_v.shape, 0)
    zero = jnp.zeros(place_v.shape, jnp.int32)
    owners, slots, before = zero, zero, zero
    for b in range(nblk):
        owners = jnp.where(lane == b, owner[b], owners)
        slots = jnp.where(lane == b, owner_slot[b], slots)
    for b in range(nblk):
        before = before + jnp.where(owners > owner[b], 1, 0)
    spot = before + slots
    plane_v = spot & (REPS - 1)
    sorted_v = plane_v * PER_PLANE + (spot >> 2)
    place_v[...] = jnp.where(line == 0, sorted_v, plane_v * CHIPS + (owners >> 1))
    to_scalar = pltpu.make_async_copy(place_v, place, sem_in.at[4])
    to_scalar.start()
    to_scalar.wait()
    order_v, dest_v = zero, zero
    slot = holder = mine = have = jnp.int32(0)
    for b in range(nblk):
        at, site = place[0, b], place[1, b]
        order_v = jnp.where(lane == at, b, order_v)
        dest_v = jnp.where(lane == site, at & (PER_PLANE - 1), dest_v)
        here = site == x * CHIPS + chip
        own = here & (owner[b] == f)
        holder = jnp.where(here, owner[b] & 1, holder)
        slot = jnp.where(own, owner_slot[b], slot)
        mine = jnp.where(own, b, mine)
        have = jnp.where(own, 1, have)
    inverse_v[...] = jnp.where(line == 0, order_v, dest_v)
    to_scalar = pltpu.make_async_copy(inverse_v, inverse, sem_in.at[5])
    to_scalar.start()
    to_scalar.wait()
    _, x_right, x_far, x_left = reps

    def stage(k):
        def body(t, _):
            xs[k, t] = grad[inverse[0, t], :, k * quarter : (k + 1) * quarter]
            return 0

        lax.fori_loop(0, nblk, body, 0, unroll=4)

    def x_copy(k, n, src, dst, to):
        i = k * 6 + n
        return pltpu.make_async_remote_copy(
            src, dst, x_send.at[i], x_recv.at[i], device_id=(f, to), device_id_type=MESH
        )

    def x_copies(k):
        far, near_r, near_l = x_far * PER_PLANE, x_right * PER_PLANE, x_left * PER_PLANE
        return (
            x_copy(k, 0, xs.at[k, pl.ds(far, HALF)], a_in.at[0, k], x_right),
            x_copy(k, 1, xs.at[k, pl.ds(far + HALF, HALF)], a_in.at[1, k], x_left),
            x_copy(k, 2, xs.at[k, pl.ds(near_r + HALF, HALF)], b_in.at[0, k], x_right),
            x_copy(k, 3, xs.at[k, pl.ds(near_l, HALF)], b_in.at[1, k], x_left),
            x_copy(k, 4, c_out.at[0, k], c_in.at[0, k], x_right),
            x_copy(k, 5, c_out.at[1, k], c_in.at[1, k], x_left),
        )

    xc = [x_copies(k) for k in range(REPS)]

    def first(k):
        xc[k][0].start()
        xc[k][1].start()

    def second(k):
        xc[k][2].start()
        xc[k][3].start()

    def wide(v):
        return v.astype(jnp.float32)

    def merge(k):
        for side, at in ((0, x_right * PER_PLANE), (1, x_left * PER_PLANE + HALF)):
            xc[k][side].wait_recv()

            def body(j, _):
                c_out[side, k, j] = (wide(xs[k, at + j]) + wide(a_in[side, k, j])).astype(jnp.bfloat16)
                return 0

            lax.fori_loop(0, HALF, body, 0, unroll=True)
            xc[k][4 + side].start()

    def finish(k):
        for n in (2, 3, 4, 5):
            xc[k][n].wait_recv()
        for lo, from_l, from_r in ((0, c_in, b_in), (HALF, b_in, c_in)):

            def body(j, _):
                total = wide(xs[k, x * PER_PLANE + lo + j]) + wide(from_l[0, k, j]) + wide(from_r[1, k, j])
                summed[k, lo + j] = total.astype(jnp.bfloat16)
                return 0

            lax.fori_loop(0, HALF, body, 0, unroll=True)

    def forward(k):
        for to in chips[1:]:
            f_out[k, to] = summed[k, inverse[1, x * CHIPS + to]]
            pltpu.make_async_remote_copy(
                f_out.at[k, to], g_in.at[k, chip, core], f_send.at[k], f_recv.at[k],
                device_id=(to * 2 + core, x), device_id_type=MESH,
            ).start()
        g_in[k, chip, core] = summed[k, inverse[1, x * CHIPS + chip]]

    def many(ref, send, recv):
        return pltpu.make_async_remote_copy(
            ref, ref, send, recv, device_id=(sibling, x), device_id_type=MESH
        )

    swaps = [
        pltpu.make_async_remote_copy(
            g_in.at[k, :, core], g_in.at[k, :, core], d_send.at[k], d_recv.at[k],
            device_id=(sibling, x), device_id_type=MESH,
        )
        for k in range(REPS)
    ]

    def swap(k):
        many(f_out.at[k, pl.ds(0, CHIPS - 1)], f_send.at[k], f_recv.at[k]).wait_recv()
        swaps[k].start()

    tile = width // 2

    def left_mul(k):
        swaps[k].wait_recv()

        def body(i, _):
            at = pl.multiple_of(i * tile, tile)
            part = jnp.dot(
                left[slot, pl.ds(at, tile), :], g_in[k].reshape(width, quarter),
                preferred_element_type=jnp.float32,
            )
            lp[pl.ds(at, tile), k * quarter : (k + 1) * quarter] = part.astype(jnp.bfloat16)
            return 0

        lax.fori_loop(0, width // tile, body, 0)

    loads[0].wait()
    stage(0)
    pl.semaphore_wait(barrier, CHIPS * REPS)
    first(0)
    second(0)
    stage(1)
    first(1)
    merge(0)
    second(1)
    stage(2)
    first(2)
    merge(1)
    second(2)
    finish(0)
    forward(0)
    stage(3)
    first(3)
    merge(2)
    second(3)
    finish(1)
    forward(1)
    loads[1].wait()
    swap(0)
    merge(3)
    left_mul(0)
    finish(2)
    forward(2)
    swap(1)
    left_mul(1)
    finish(3)
    forward(3)

    moments = []
    for i in range(1, REPS):
        to = reps[i]
        moments.append(
            pltpu.make_async_remote_copy(
                summed.at[to], mom_in.at[x], m_send.at[i], m_recv.at[i],
                device_id=(f, to), device_id_type=MESH,
            )
        )
        moments[-1].start()
    mom_in[x] = summed[x]

    swap(2)
    left_mul(2)

    loads[2].wait()
    swap(3)
    left_mul(3)

    halves = width // tile
    chips_per = CHIPS // halves

    def right_mul(i, squares):
        cols = pl.ds(pl.multiple_of(reps[i] * quarter, quarter), quarter)

        def body(n, acc):
            at = pl.multiple_of(n * tile, tile)
            part = jnp.dot(
                lp[pl.ds(at, tile), :], right[slot, :, cols], preferred_element_type=jnp.float32
            )
            pbs[i][core, pl.ds(n * chips_per, chips_per)] = part.astype(jnp.bfloat16).reshape(
                chips_per, 2, rows, quarter
            )
            return acc + jnp.sum(part * part, axis=0, keepdims=True)

        return lax.fori_loop(0, halves, body, squares)

    trades = [
        pltpu.make_async_remote_copy(
            pb.at[core, :, 1 - core], pb.at[core, :, 1 - core], p_send.at[i], p_recv.at[i],
            device_id=(sibling, x), device_id_type=MESH,
        )
        for i, pb in enumerate(pbs)
    ]

    def send_back(i):
        pb = pbs[i]
        trades[i].wait_recv()
        for to in chips[1:] if i == 0 else chips:
            ret[i, to] = pb[holder, to, core]
            pltpu.make_async_remote_copy(
                ret.at[i, to], back.at[x * CHIPS + chip], u_send.at[0], u_recv.at[0],
                device_id=(to * 2 + core, reps[i]), device_id_type=MESH,
            ).start()
        if i == 0:
            back[x * CHIPS + chip] = pb[holder, chip, core]

    squares = jnp.zeros((1, quarter), jnp.float32)
    for i in range(REPS):
        squares = right_mul(i, squares)
        trades[i].start()
        if i in (1, 2):
            send_back(i - 1)

    loads[3].wait()
    for copy in moments:
        copy.wait_recv()

    at_lane = lax.broadcasted_iota(jnp.int32, (1, 128), 1)

    def moment(b, sums):
        t = place[0, b]
        s = wide(mom_in[t >> 3, t & (PER_PLANE - 1)])
        new = 0.99 * sm[b] + 0.01 * s * s
        nm[b] = new
        adam = s / (jnp.sqrt(new) + 1e-08)
        sq = jnp.sum(adam * adam, axis=0, keepdims=True)
        return jnp.where(at_lane == b, jnp.sum(sq, axis=1, keepdims=True), sums)

    owned = (at_lane == nblk + mine) & (have == 1)
    own_sums = jnp.where(owned, jnp.sum(squares, axis=1, keepdims=True), 0.0)
    own_sums = lax.fori_loop(0, nblk, moment, own_sums, unroll=4)
    ad_1[pl.ds(0, 1), :] = own_sums
    sums_chip = pltpu.make_async_remote_copy(
        ad_1.at[pl.ds(0, 1)], ad_1.at[pl.ds(8, 1)], s_send.at[0], s_recv.at[0],
        device_id=(sibling, x), device_id_type=MESH,
    )
    sums_chip.start()
    store_nm = pltpu.make_async_copy(nm, nm_hbm, sem_out.at[0])
    store_nm.start()
    sums_chip.wait_recv()
    ad_2[x * CHIPS + chip] = jnp.broadcast_to(own_sums + ad_1[pl.ds(8, 1), :], ad_2.shape[1:])
    for i in range(1, CHIPS * REPS):
        pltpu.make_async_remote_copy(
            ad_2.at[x * CHIPS + chip], ad_2.at[x * CHIPS + chip], s_send.at[1], s_recv.at[1],
            device_id=(chips[i // REPS] * 2 + core, reps[i % REPS]), device_id_type=MESH,
        ).start()
    send_back(2)
    send_back(3)

    many(ad_2.at[pl.ds(0, CHIPS * REPS - 1)], s_send.at[1], s_recv.at[1]).wait_recv()
    total = jnp.sum(ad_2[...], axis=0)
    line = lax.broadcasted_iota(jnp.int32, (nblk, 128), 0)
    lane = lax.broadcasted_iota(jnp.int32, (nblk, 128), 1)
    total = jnp.broadcast_to(total[:1, :], (nblk, 128))
    area = width * width
    adam_mean = jnp.sum(jnp.where(lane == line, total, 0.0), axis=1, keepdims=True) / area
    prod_mean = jnp.sum(jnp.where(lane == line + nblk, total, 0.0), axis=1, keepdims=True) / area
    scale = jnp.sqrt(adam_mean) / jnp.sqrt(prod_mean + 1e-06)
    factor[...] = jnp.broadcast_to(scale, factor.shape)

    many(back.at[pl.ds(0, CHIPS * REPS - 1)], u_send.at[0], u_recv.at[0]).wait_recv()

    def collect(b, _):
        by = factor[pl.ds(b, 1), :]
        by = jnp.concatenate([by, by], axis=1)
        upd[b] = (wide(back[place[1, b]]) * by).astype(jnp.bfloat16)
        return 0

    lax.fori_loop(0, nblk, collect, 0, unroll=2)
    store_upd = pltpu.make_async_copy(upd, upd_hbm, sem_out.at[1])
    store_upd.start()

    for k in range(REPS):
        for copy in xc[k]:
            copy.wait_send()
        many(f_out.at[k, pl.ds(0, CHIPS - 1)], f_send.at[k], f_recv.at[k]).wait_send()
        swaps[k].wait_send()
        trades[k].wait_send()
    for copy in moments + [sums_chip]:
        copy.wait_send()
    many(ad_2.at[pl.ds(0, CHIPS * REPS - 1)], s_send.at[1], s_recv.at[1]).wait_send()
    many(back.at[pl.ds(0, CHIPS * REPS - 1)], u_send.at[0], u_recv.at[0]).wait_send()
    store_nm.wait()
    store_upd.wait()


def one_kernel(grad, second_moment, left_factor, right_factor, block_owner, block_slot):
    nblk, rows, width = grad.shape
    slots = left_factor.shape[0]
    quarter = width // REPS
    bf, f32 = jnp.bfloat16, jnp.float32
    piece = (rows, quarter)
    any_spec = pl.BlockSpec(memory_space=pl.ANY)
    vmem = pltpu.VMEM
    dma = pltpu.SemaphoreType.DMA
    return pl.pallas_call(
        step_kernel,
        out_shape=(
            jax.ShapeDtypeStruct((nblk, rows, quarter), bf),
            jax.ShapeDtypeStruct((nblk, rows, quarter), f32),
        ),
        in_specs=[pl.BlockSpec(memory_space=pltpu.SMEM)] * 2 + [any_spec] * 4,
        out_specs=(any_spec, any_spec),
        scratch_shapes=[
            vmem((nblk, rows, width), bf),
            vmem((nblk, rows, quarter), f32),
            vmem((slots, width, width), bf),
            vmem((slots, width, width), bf),
            vmem((REPS, nblk) + piece, bf),
            vmem((2, REPS, HALF) + piece, bf),
            vmem((2, REPS, HALF) + piece, bf),
            vmem((2, REPS, HALF) + piece, bf),
            vmem((2, REPS, HALF) + piece, bf),
            vmem((REPS, PER_PLANE) + piece, bf),
            vmem((REPS, CHIPS) + piece, bf),
            vmem((REPS, CHIPS, 2) + piece, bf),
            vmem((width, width), bf),
        ]
        + [vmem((2, CHIPS, 2) + piece, bf)] * REPS
        + [
            vmem((REPS, CHIPS) + piece, bf),
            vmem((REPS * CHIPS,) + piece, bf),
            vmem((REPS, PER_PLANE) + piece, bf),
            vmem((nblk,) + piece, f32),
            vmem((nblk,) + piece, bf),
            vmem((16, 128), f32),
            vmem((REPS * CHIPS, 8, 128), f32),
            vmem((nblk, 128), f32),
            vmem((8, 128), jnp.int32),
            pltpu.SMEM((8, 128), jnp.int32),
            vmem((8, 128), jnp.int32),
            pltpu.SMEM((8, 128), jnp.int32),
            dma((6,)),
            dma((2,)),
            dma((REPS * 6,)),
            dma((REPS * 6,)),
        ]
        + [dma((REPS,))] * 6
        + [dma((1,)), dma((1,)), dma((REPS,)), dma((REPS,)), dma((2,)), dma((2,))],
        compiler_params=pltpu.CompilerParams(
            collective_id=0, has_side_effects=True, vmem_limit_bytes=58 << 20
        ),
        cost_estimate=pl.CostEstimate(
            flops=4 * width**3, bytes_accessed=18 << 20, transcendentals=nblk * rows * quarter
        ),
        name="shampoo_step",
    )(block_owner, block_slot, grad, second_moment, left_factor, right_factor)


def crowded(block_owner, block_slot):
    bit = jnp.left_shift(jnp.int32(1), block_owner)
    other = jnp.left_shift(jnp.int32(1), block_owner ^ 1)
    third = jnp.sum(jnp.where(block_slot == 2, bit, 0))
    second = jnp.sum(jnp.where(block_slot == 1, other, 0))
    return (third & second) != 0


def ring_sum(value, axis):
    count = lax.axis_size(axis)
    step = 1
    while step < count:
        value = value + lax.ppermute(value, axis, [(i, i ^ step) for i in range(count)])
        step *= 2
    return value


def general(grad_partial, second_moment, left_factor, right_factor, block_owner, block_slot):
    slot_count = left_factor.shape[0]
    row_count = grad_partial.shape[2]
    full_width = grad_partial.shape[3]
    rep_count = lax.axis_size("rep")
    owner_count = lax.axis_size("fsdp")
    owner_index = lax.axis_index("fsdp")
    rep_index = lax.axis_index("rep")
    quarter = full_width // rep_count
    slot_range = jnp.arange(slot_count, dtype=jnp.int32)
    owner_range = jnp.arange(owner_count, dtype=jnp.int32)
    selector = (
        (block_slot[None, None, :] == slot_range[:, None, None])
        & (block_owner[None, None, :] == owner_range[None, :, None])
    ).astype(jnp.bfloat16)
    owned = (
        (block_slot[None, :] == slot_range[:, None]) & (block_owner[None, :] == owner_index)
    ).astype(jnp.float32)
    summed = ring_sum(grad_partial[0].astype(jnp.float32), "rep")
    column = lax.dynamic_slice_in_dim(summed, rep_index * quarter, quarter, 2)
    new_moment = 0.99 * second_moment + 0.01 * column * column
    adam = column / (jnp.sqrt(new_moment) + 1e-08)
    partial_squares = jnp.sum(adam * adam, axis=(1, 2))
    total_squares = ring_sum(ring_sum(partial_squares, "rep"), "fsdp")
    adam_rms = jnp.sqrt(total_squares / (full_width * full_width))
    slot_rms = jnp.sum(owned * adam_rms[None, :], axis=1)
    grad_bf = summed.astype(jnp.bfloat16)
    outbound = jnp.einsum(
        "kdn,nrc->kdrc", selector, grad_bf, preferred_element_type=jnp.float32
    ).astype(jnp.bfloat16)
    outbound = outbound.reshape(slot_count, owner_count * row_count, full_width)
    inbound = lax.all_to_all(outbound, "fsdp", split_axis=1, concat_axis=1, tiled=True)
    left_prod = jnp.einsum(
        "kij,kjc->kic", left_factor, inbound, preferred_element_type=jnp.float32
    ).astype(jnp.bfloat16)
    product = jnp.einsum(
        "kij,kjc->kic", left_prod, right_factor, preferred_element_type=jnp.float32
    )
    prod_mean = jnp.mean(product * product, axis=(1, 2))
    graft = slot_rms / jnp.sqrt(prod_mean + 1e-06)
    scaled = (product * graft[:, None, None]).astype(jnp.bfloat16)
    returned = lax.all_to_all(scaled, "fsdp", split_axis=1, concat_axis=1, tiled=True)
    returned = lax.dynamic_slice_in_dim(returned, rep_index * quarter, quarter, 2)
    returned = returned.reshape(slot_count, owner_count, row_count, quarter)
    update = jnp.einsum(
        "kdn,kdrc->nrc", selector, returned, preferred_element_type=jnp.float32
    ).astype(jnp.bfloat16)
    return (update, new_moment)


def per_device(grad_partial, second_moment, left_factor, right_factor, block_owner, block_slot):
    def direct(gp, sm, lf, rf, owner, slot):
        return one_kernel(gp[0], sm, lf, rf, owner, slot)

    return lax.cond(
        crowded(block_owner, block_slot), general, direct,
        grad_partial, second_moment, left_factor, right_factor, block_owner, block_slot,
    )


def solution(mesh):
    placed = (
        P("rep", None, "fsdp", None),
        P(None, "fsdp", "rep"),
        P("fsdp", None, None),
        P("fsdp", None, None),
        P(),
        P(),
    )
    return jax.shard_map(
        per_device,
        mesh=mesh,
        in_specs=placed,
        out_specs=(P(None, "fsdp", "rep"), P(None, "fsdp", "rep")),
        check_vma=False,
    )
```

```python
import functools

import jax
import jax.numpy as jnp
from jax import lax
from jax.experimental import pallas as pl
from jax.experimental.pallas import tpu as pltpu
from jax.sharding import PartitionSpec as P

MESH = pl.DeviceIdType.MESH
REPS = 4
CHIPS = 16
SIDE = 4
PER_PLANE = 8
HALF = PER_PLANE // 2
CUTS = 4


def step_kernel(
    owner, owner_slot, g_hbm, sm_hbm, l_hbm, r_hbm, upd_hbm, nm_hbm,
    grad, sm, left, right, xs, a_in, b_in, c_in, c_out, summed, f_out, g_in,
    lp, pb0, pb1, pb2, pb3, ret, back, mom_in, nm, upd,
    ad_1, ad_x, ad_p, factor, place_v, place, inverse_v, inverse,
    sem_in, sem_out, x_send, x_recv, f_send, f_recv, d_send, d_recv,
    p_send, p_recv, u_send, u_recv, m_send, m_recv, s_send, s_recv,
):
    pbs = (pb0, pb1, pb2, pb3)
    f = lax.axis_index("fsdp")
    x = lax.axis_index("rep")
    core = f % 2
    chip = f // 2
    cy = chip // SIDE
    cz = chip % SIDE
    sibling = f + 1 - 2 * core
    nblk, rows, width = grad.shape
    quarter = width // REPS
    cut = width // CUTS
    per_quarter = CUTS // REPS

    chips = [
        lax.rem(cy + i // SIDE, SIDE) * SIDE + lax.rem(cz + i % SIDE, SIDE) for i in range(CHIPS)
    ]
    reps = [lax.rem(x + i, REPS) for i in range(REPS)]

    loads = [
        pltpu.make_async_copy(src, dst, sem_in.at[i])
        for i, (src, dst) in enumerate(
            ((g_hbm, grad), (l_hbm, left), (r_hbm, right), (sm_hbm, sm))
        )
    ]
    for load in loads:
        load.start()

    barrier = pltpu.get_barrier_semaphore()

    for i in range(1, CHIPS * REPS):
        to = (chips[i // REPS] * 2 + core, reps[i % REPS])
        pl.semaphore_signal(barrier, inc=1, device_id=to, device_id_type=MESH)
    pl.semaphore_signal(barrier, inc=1, device_id=(sibling, x), device_id_type=MESH)

    lane = lax.broadcasted_iota(jnp.int32, place_v.shape, 1)
    line = lax.broadcasted_iota(jnp.int32, place_v.shape, 0)
    zero = jnp.zeros(place_v.shape, jnp.int32)
    owners, slots, before = zero, zero, zero
    for b in range(nblk):
        owners = jnp.where(lane == b, owner[b], owners)
        slots = jnp.where(lane == b, owner_slot[b], slots)
    for b in range(nblk):
        before = before + jnp.where(owners > owner[b], 1, 0)
    spot = before + slots
    plane_v = spot & (REPS - 1)
    sorted_v = plane_v * PER_PLANE + (spot >> 2)
    place_v[...] = jnp.where(line == 0, sorted_v, plane_v * CHIPS + (owners >> 1))
    to_scalar = pltpu.make_async_copy(place_v, place, sem_in.at[4])
    to_scalar.start()
    to_scalar.wait()
    order_v, dest_v = zero, zero
    slot = holder = mine = have = jnp.int32(0)
    for b in range(nblk):
        at, site = place[0, b], place[1, b]
        order_v = jnp.where(lane == at, b, order_v)
        dest_v = jnp.where(lane == site, at & (PER_PLANE - 1), dest_v)
        here = site == x * CHIPS + chip
        own = here & (owner[b] == f)
        holder = jnp.where(here, owner[b] & 1, holder)
        slot = jnp.where(own, owner_slot[b], slot)
        mine = jnp.where(own, b, mine)
        have = jnp.where(own, 1, have)
    inverse_v[...] = jnp.where(line == 0, order_v, dest_v)
    to_scalar = pltpu.make_async_copy(inverse_v, inverse, sem_in.at[5])
    to_scalar.start()
    to_scalar.wait()
    _, x_right, x_far, x_left = reps

    def many(ref, send, recv):
        return pltpu.make_async_remote_copy(
            ref, ref, send, recv, device_id=(sibling, x), device_id_type=MESH
        )

    def stage(k):
        def body(t, _):
            xs[k, t] = grad[inverse[0, t], :, k * cut : (k + 1) * cut]
            return 0

        lax.fori_loop(0, nblk, body, 0, unroll=4)

    def x_copy(k, n, src, dst, to):
        return pltpu.make_async_remote_copy(
            src, dst, x_send.at[0], x_recv.at[k, min(n // 2, 1)], device_id=(f, to), device_id_type=MESH
        )

    def x_copies(k):
        far, near_r, near_l = x_far * PER_PLANE, x_right * PER_PLANE, x_left * PER_PLANE
        return (
            x_copy(k, 0, xs.at[k, pl.ds(far, HALF)], a_in.at[0, k], x_right),
            x_copy(k, 1, xs.at[k, pl.ds(far + HALF, HALF)], a_in.at[1, k], x_left),
            x_copy(k, 2, xs.at[k, pl.ds(near_r + HALF, HALF)], b_in.at[0, k], x_right),
            x_copy(k, 3, xs.at[k, pl.ds(near_l, HALF)], b_in.at[1, k], x_left),
            x_copy(k, 4, c_out.at[0, k], c_in.at[0, k], x_right),
            x_copy(k, 5, c_out.at[1, k], c_in.at[1, k], x_left),
        )

    xc = [x_copies(k) for k in range(CUTS)]

    def first(k):
        xc[k][0].start()
        xc[k][1].start()

    def second(k):
        xc[k][2].start()
        xc[k][3].start()

    def wide(v):
        return v.astype(jnp.float32)

    def merge(k):
        many(xs.at[k, pl.ds(0, PER_PLANE)], x_send.at[0], x_recv.at[k, 0]).wait_recv()
        for side, at in ((0, x_right * PER_PLANE), (1, x_left * PER_PLANE + HALF)):

            def body(j, _):
                c_out[side, k, j] = (wide(xs[k, at + j]) + wide(a_in[side, k, j])).astype(jnp.bfloat16)
                return 0

            lax.fori_loop(0, HALF, body, 0, unroll=True)
            xc[k][4 + side].start()

    def finish(k):
        many(xs.at[k, pl.ds(0, 2 * PER_PLANE)], x_send.at[0], x_recv.at[k, 1]).wait_recv()
        for lo, from_l, from_r in ((0, c_in, b_in), (HALF, b_in, c_in)):

            def body(j, _):
                total = wide(xs[k, x * PER_PLANE + lo + j]) + wide(from_l[0, k, j]) + wide(from_r[1, k, j])
                summed[k, lo + j] = total.astype(jnp.bfloat16)
                return 0

            lax.fori_loop(0, HALF, body, 0, unroll=True)

    def forward(k):
        for to in chips[1:]:
            f_out[k, to] = summed[k, inverse[1, x * CHIPS + to]]
            pltpu.make_async_remote_copy(
                f_out.at[k, to], g_in.at[k, chip, core], f_send.at[0], f_recv.at[k],
                device_id=(to * 2 + core, x), device_id_type=MESH,
            ).start()
        g_in[k, chip, core] = summed[k, inverse[1, x * CHIPS + chip]]

    swaps = [
        pltpu.make_async_remote_copy(
            g_in.at[k, :, core], g_in.at[k, :, core], d_send.at[0], d_recv.at[k],
            device_id=(sibling, x), device_id_type=MESH,
        )
        for k in range(CUTS)
    ]

    def swap(k):
        many(f_out.at[k, pl.ds(0, CHIPS - 1)], f_send.at[0], f_recv.at[k]).wait_recv()
        swaps[k].start()

    def left_mul(m):
        parts = range(m * per_quarter, (m + 1) * per_quarter)
        for k in parts:
            swaps[k].wait_recv()

        block = jnp.concatenate([g_in[k].reshape(width, cut) for k in parts], axis=1)
        part = jnp.dot(left[slot], block, preferred_element_type=jnp.float32)
        lp[:, m * quarter : (m + 1) * quarter] = part.astype(jnp.bfloat16)

    loads[0].wait()
    stage(0)
    pl.semaphore_wait(barrier, CHIPS * REPS)
    first(0)
    second(0)
    for k in range(1, CUTS + 1):
        if k < CUTS:
            stage(k)
            first(k)
        merge(k - 1)
        if k < CUTS:
            second(k)
        if k == CUTS:
            swap(0)
        if k >= 2:
            finish(k - 2)
            forward(k - 2)
    loads[1].wait()
    left_mul(0)
    swap(1)
    left_mul(1)
    finish(CUTS - 1)
    forward(CUTS - 1)

    for i in range(1, REPS):
        to = reps[i]
        pltpu.make_async_remote_copy(
            summed.at[pl.ds(to * per_quarter, per_quarter)], mom_in.at[x], m_send.at[0], m_recv.at[0],
            device_id=(f, to), device_id_type=MESH,
        ).start()
    mom_in[x] = summed[pl.ds(x * per_quarter, per_quarter)]

    swap(2)
    left_mul(2)
    loads[2].wait()
    swap(3)
    left_mul(3)

    def right_mul(i, squares):
        cols = pl.ds(pl.multiple_of(reps[i] * quarter, quarter), quarter)
        part = jnp.dot(lp[...], right[slot, :, cols], preferred_element_type=jnp.float32)
        pbs[i][core] = part.astype(jnp.bfloat16).reshape(CHIPS, 2, rows, quarter)
        return squares + jnp.sum(part * part, axis=0, keepdims=True)

    trades = [
        pltpu.make_async_remote_copy(
            pb.at[core, :, 1 - core], pb.at[core, :, 1 - core], p_send.at[0], p_recv.at[i],
            device_id=(sibling, x), device_id_type=MESH,
        )
        for i, pb in enumerate(pbs)
    ]

    def send_back(*which):
        for i in which:
            trades[i].wait_recv()
        for to in chips:
            for i in which:
                if i == 0 and to is chips[0]:
                    back[x * CHIPS + chip] = pbs[i][holder, chip, core]
                    continue
                ret[i, to] = pbs[i][holder, to, core]
                pltpu.make_async_remote_copy(
                    ret.at[i, to], back.at[x * CHIPS + chip], u_send.at[0], u_recv.at[0],
                    device_id=(to * 2 + core, reps[i]), device_id_type=MESH,
                ).start()

    squares = jnp.zeros((1, quarter), jnp.float32)
    for i in (2, 0, 1, 3):
        squares = right_mul(i, squares)
        trades[i].start()
        if i == 1:
            send_back(2, 0)

    loads[3].wait()
    moments = many(xs.at[0, pl.ds(0, (REPS - 1) * PER_PLANE)], m_send.at[0], m_recv.at[0])
    moments.wait_recv()

    at_lane = lax.broadcasted_iota(jnp.int32, (1, 128), 1)

    def moment(b, sums):
        t = place[0, b]
        sq = jnp.zeros((1, cut), jnp.float32)
        for h in range(per_quarter):
            s = wide(mom_in[t >> 3, h, t & (PER_PLANE - 1)])
            at = slice(h * cut, (h + 1) * cut)
            new = 0.99 * sm[b, :, at] + 0.01 * s * s
            nm[b, :, at] = new
            adam = s / (jnp.sqrt(new) + 1e-08)
            sq = sq + jnp.sum(adam * adam, axis=0, keepdims=True)
        return jnp.where(at_lane == b, jnp.sum(sq, axis=1, keepdims=True), sums)

    owned = (at_lane == nblk + mine) & (have == 1)
    own_sums = jnp.where(owned, jnp.sum(squares, axis=1, keepdims=True), 0.0)
    own_sums = lax.fori_loop(0, nblk, moment, own_sums, unroll=4)
    ad_1[pl.ds(0, 1), :] = own_sums
    sums_chip = pltpu.make_async_remote_copy(
        ad_1.at[pl.ds(0, 1)], ad_1.at[pl.ds(8, 1)], s_send.at[0], s_recv.at[0],
        device_id=(sibling, x), device_id_type=MESH,
    )
    sums_chip.start()
    store_nm = pltpu.make_async_copy(nm, nm_hbm, sem_out.at[0])
    store_nm.start()
    sums_chip.wait_recv()
    ad_x[x, pl.ds(0, 1), :] = own_sums + ad_1[pl.ds(8, 1), :]
    for i in range(1, REPS):
        pltpu.make_async_remote_copy(
            ad_x.at[x, pl.ds(0, 1)], ad_x.at[x, pl.ds(0, 1)], s_send.at[1], s_recv.at[1],
            device_id=(f, reps[i]), device_id_type=MESH,
        ).start()
    send_back(1)
    sums_x = many(ad_x.at[pl.ds(0, REPS - 1), pl.ds(0, 1)], s_send.at[1], s_recv.at[1])
    sums_x.wait_recv()
    ad_p[chip, pl.ds(0, 1), :] = jnp.sum(ad_x[:, pl.ds(0, 1), :], axis=0)
    for to in chips[1:]:
        pltpu.make_async_remote_copy(
            ad_p.at[chip, pl.ds(0, 1)], ad_p.at[chip, pl.ds(0, 1)], s_send.at[2], s_recv.at[2],
            device_id=(to * 2 + core, x), device_id_type=MESH,
        ).start()
    send_back(3)

    sums_plane = many(ad_p.at[pl.ds(0, CHIPS - 1), pl.ds(0, 1)], s_send.at[2], s_recv.at[2])
    sums_plane.wait_recv()
    total = jnp.sum(ad_p[:, pl.ds(0, 1), :], axis=0)
    line = lax.broadcasted_iota(jnp.int32, (nblk, 128), 0)
    lane = lax.broadcasted_iota(jnp.int32, (nblk, 128), 1)
    total = jnp.broadcast_to(total, (nblk, 128))
    area = width * width
    adam_mean = jnp.sum(jnp.where(lane == line, total, 0.0), axis=1, keepdims=True) / area
    prod_mean = jnp.sum(jnp.where(lane == line + nblk, total, 0.0), axis=1, keepdims=True) / area
    scale = jnp.sqrt(adam_mean) / jnp.sqrt(prod_mean + 1e-06)
    factor[...] = jnp.broadcast_to(scale, factor.shape)

    many(back.at[pl.ds(0, CHIPS * REPS - 1)], u_send.at[0], u_recv.at[0]).wait_recv()

    def collect(b, _):
        by = factor[pl.ds(b, 1), :]
        by = jnp.concatenate([by, by], axis=1)
        upd[b] = (wide(back[place[1, b]]) * by).astype(jnp.bfloat16)
        return 0

    lax.fori_loop(0, nblk, collect, 0, unroll=2)
    store_upd = pltpu.make_async_copy(upd, upd_hbm, sem_out.at[1])
    store_upd.start()

    many(xs.at[:, pl.ds(0, 6 * HALF)], x_send.at[0], x_recv.at[0, 0]).wait_send()
    many(f_out.at[:, pl.ds(0, CHIPS - 1)], f_send.at[0], f_recv.at[0]).wait_send()
    many(f_out, d_send.at[0], d_recv.at[0]).wait_send()
    many(ret, p_send.at[0], p_recv.at[0]).wait_send()
    for copy in (moments, sums_chip, sums_x, sums_plane):
        copy.wait_send()
    many(back.at[pl.ds(0, CHIPS * REPS - 1)], u_send.at[0], u_recv.at[0]).wait_send()
    store_nm.wait()
    store_upd.wait()


def one_kernel(grad, second_moment, left_factor, right_factor, block_owner, block_slot):
    nblk, rows, width = grad.shape
    slots = left_factor.shape[0]
    quarter = width // REPS
    bf, f32 = jnp.bfloat16, jnp.float32
    piece = (rows, quarter)
    part = (rows, width // CUTS)
    any_spec = pl.BlockSpec(memory_space=pl.ANY)
    vmem = pltpu.VMEM
    dma = pltpu.SemaphoreType.DMA
    return pl.pallas_call(
        step_kernel,
        out_shape=(
            jax.ShapeDtypeStruct((nblk, rows, quarter), bf),
            jax.ShapeDtypeStruct((nblk, rows, quarter), f32),
        ),
        in_specs=[pl.BlockSpec(memory_space=pltpu.SMEM)] * 2 + [any_spec] * 4,
        out_specs=(any_spec, any_spec),
        scratch_shapes=[
            vmem((nblk, rows, width), bf),
            vmem((nblk, rows, quarter), f32),
            vmem((slots, width, width), bf),
            vmem((slots, width, width), bf),
            vmem((CUTS, nblk) + part, bf),
            vmem((2, CUTS, HALF) + part, bf),
            vmem((2, CUTS, HALF) + part, bf),
            vmem((2, CUTS, HALF) + part, bf),
            vmem((2, CUTS, HALF) + part, bf),
            vmem((CUTS, PER_PLANE) + part, bf),
            vmem((CUTS, CHIPS) + part, bf),
            vmem((CUTS, CHIPS, 2) + part, bf),
            vmem((width, width), bf),
        ]
        + [vmem((2, CHIPS, 2) + piece, bf)] * REPS
        + [
            vmem((REPS, CHIPS) + piece, bf),
            vmem((REPS * CHIPS,) + piece, bf),
            vmem((REPS, CUTS // REPS, PER_PLANE) + part, bf),
            vmem((nblk,) + piece, f32),
            vmem((nblk,) + piece, bf),
            vmem((16, 128), f32),
            vmem((REPS, 8, 128), f32),
            vmem((CHIPS, 8, 128), f32),
            vmem((nblk, 128), f32),
            vmem((8, 128), jnp.int32),
            pltpu.SMEM((8, 128), jnp.int32),
            vmem((8, 128), jnp.int32),
            pltpu.SMEM((8, 128), jnp.int32),
            dma((6,)),
            dma((2,)),
            dma((1,)),
            dma((CUTS, 2)),
            dma((1,)),
            dma((CUTS,)),
            dma((1,)),
            dma((CUTS,)),
            dma((1,)),
            dma((REPS,)),
        ]
        + [dma((1,))] * 4
        + [dma((3,))] * 2,
        compiler_params=pltpu.CompilerParams(
            collective_id=0, has_side_effects=True, vmem_limit_bytes=58 << 20
        ),
        cost_estimate=pl.CostEstimate(
            flops=4 * width**3, bytes_accessed=18 << 20, transcendentals=nblk * rows * quarter
        ),
        name="shampoo_step",
    )(block_owner, block_slot, grad, second_moment, left_factor, right_factor)


def crowded(block_owner, block_slot):
    bit = jnp.left_shift(jnp.int32(1), block_owner)
    other = jnp.left_shift(jnp.int32(1), block_owner ^ 1)
    third = jnp.sum(jnp.where(block_slot == 2, bit, 0))
    second = jnp.sum(jnp.where(block_slot == 1, other, 0))
    return (third & second) != 0


def ring_sum(value, axis):
    count = lax.axis_size(axis)
    step = 1
    while step < count:
        value = value + lax.ppermute(value, axis, [(i, i ^ step) for i in range(count)])
        step *= 2
    return value


def general(grad_partial, second_moment, left_factor, right_factor, block_owner, block_slot):
    slot_count = left_factor.shape[0]
    row_count = grad_partial.shape[2]
    full_width = grad_partial.shape[3]
    rep_count = lax.axis_size("rep")
    owner_count = lax.axis_size("fsdp")
    owner_index = lax.axis_index("fsdp")
    rep_index = lax.axis_index("rep")
    quarter = full_width // rep_count
    slot_range = jnp.arange(slot_count, dtype=jnp.int32)
    owner_range = jnp.arange(owner_count, dtype=jnp.int32)
    selector = (
        (block_slot[None, None, :] == slot_range[:, None, None])
        & (block_owner[None, None, :] == owner_range[None, :, None])
    ).astype(jnp.bfloat16)
    owned = (
        (block_slot[None, :] == slot_range[:, None]) & (block_owner[None, :] == owner_index)
    ).astype(jnp.float32)
    summed = ring_sum(grad_partial[0].astype(jnp.float32), "rep")
    column = lax.dynamic_slice_in_dim(summed, rep_index * quarter, quarter, 2)
    new_moment = 0.99 * second_moment + 0.01 * column * column
    adam = column / (jnp.sqrt(new_moment) + 1e-08)
    partial_squares = jnp.sum(adam * adam, axis=(1, 2))
    total_squares = ring_sum(ring_sum(partial_squares, "rep"), "fsdp")
    adam_rms = jnp.sqrt(total_squares / (full_width * full_width))
    slot_rms = jnp.sum(owned * adam_rms[None, :], axis=1)
    grad_bf = summed.astype(jnp.bfloat16)
    outbound = jnp.einsum(
        "kdn,nrc->kdrc", selector, grad_bf, preferred_element_type=jnp.float32
    ).astype(jnp.bfloat16)
    outbound = outbound.reshape(slot_count, owner_count * row_count, full_width)
    inbound = lax.all_to_all(outbound, "fsdp", split_axis=1, concat_axis=1, tiled=True)
    left_prod = jnp.einsum(
        "kij,kjc->kic", left_factor, inbound, preferred_element_type=jnp.float32
    ).astype(jnp.bfloat16)
    product = jnp.einsum(
        "kij,kjc->kic", left_prod, right_factor, preferred_element_type=jnp.float32
    )
    prod_mean = jnp.mean(product * product, axis=(1, 2))
    graft = slot_rms / jnp.sqrt(prod_mean + 1e-06)
    scaled = (product * graft[:, None, None]).astype(jnp.bfloat16)
    returned = lax.all_to_all(scaled, "fsdp", split_axis=1, concat_axis=1, tiled=True)
    returned = lax.dynamic_slice_in_dim(returned, rep_index * quarter, quarter, 2)
    returned = returned.reshape(slot_count, owner_count, row_count, quarter)
    update = jnp.einsum(
        "kdn,kdrc->nrc", selector, returned, preferred_element_type=jnp.float32
    ).astype(jnp.bfloat16)
    return (update, new_moment)


def per_device(grad_partial, second_moment, left_factor, right_factor, block_owner, block_slot):
    def direct(gp, sm, lf, rf, owner, slot):
        return one_kernel(gp[0], sm, lf, rf, owner, slot)

    return lax.cond(
        crowded(block_owner, block_slot), general, direct,
        grad_partial, second_moment, left_factor, right_factor, block_owner, block_slot,
    )


def solution(mesh):
    placed = (
        P("rep", None, "fsdp", None),
        P(None, "fsdp", "rep"),
        P("fsdp", None, None),
        P("fsdp", None, None),
        P(),
        P(),
    )
    return jax.shard_map(
        per_device,
        mesh=mesh,
        in_specs=placed,
        out_specs=(P(None, "fsdp", "rep"), P(None, "fsdp", "rep")),
        check_vma=False,
    )
```

```python
import functools

import jax
import jax.numpy as jnp
from jax import lax
from jax.experimental import pallas as pl
from jax.experimental.pallas import tpu as pltpu
from jax.sharding import PartitionSpec as P

MESH = pl.DeviceIdType.MESH
REPS = 4
CHIPS = 16
SIDE = 4
PER_PLANE = 8
HALF = PER_PLANE // 2
CUTS = 4


def step_kernel(
    owner, owner_slot, g_hbm, sm_hbm, l_hbm, r_hbm, upd_hbm, nm_hbm,
    grad, sm, left, right, xs, a_in, b_in, c_in, c_out, summed, f_out, g_in,
    lp, pb0, pb1, pb2, pb3, ret, back, mom_in, nm, upd,
    ad_1, ad_x, ad_p, factor, place_v, place, inverse_v, inverse,
    sem_in, sem_out, x_send, x_recv, f_send, f_recv, d_send, d_recv,
    p_send, p_recv, u_send, u_recv, m_send, m_recv, s_send, s_recv,
):
    pbs = (pb0, pb1, pb2, pb3)
    f = lax.axis_index("fsdp")
    x = lax.axis_index("rep")
    core = f % 2
    chip = f // 2
    cy = chip // SIDE
    cz = chip % SIDE
    sibling = f + 1 - 2 * core
    nblk, rows, width = grad.shape
    quarter = width // REPS
    cut = width // CUTS
    per_quarter = CUTS // REPS

    chips = [
        lax.rem(cy + i // SIDE, SIDE) * SIDE + lax.rem(cz + i % SIDE, SIDE) for i in range(CHIPS)
    ]
    reps = [lax.rem(x + i, REPS) for i in range(REPS)]

    loads = [
        pltpu.make_async_copy(src, dst, sem_in.at[i])
        for i, (src, dst) in enumerate(
            ((g_hbm, grad), (l_hbm, left), (r_hbm, right), (sm_hbm, sm))
        )
    ]
    for load in loads:
        load.start()

    barrier = pltpu.get_barrier_semaphore()

    for i in range(1, CHIPS * REPS):
        to = (chips[i // REPS] * 2 + core, reps[i % REPS])
        pl.semaphore_signal(barrier, inc=1, device_id=to, device_id_type=MESH)
    pl.semaphore_signal(barrier, inc=1, device_id=(sibling, x), device_id_type=MESH)

    lane = lax.broadcasted_iota(jnp.int32, place_v.shape, 1)
    line = lax.broadcasted_iota(jnp.int32, place_v.shape, 0)
    zero = jnp.zeros(place_v.shape, jnp.int32)
    owners, slots, before = zero, zero, zero
    for b in range(nblk):
        owners = jnp.where(lane == b, owner[b], owners)
        slots = jnp.where(lane == b, owner_slot[b], slots)
    for b in range(nblk):
        before = before + jnp.where(owners > owner[b], 1, 0)
    spot = before + slots
    plane_v = spot & (REPS - 1)
    sorted_v = plane_v * PER_PLANE + (spot >> 2)
    place_v[...] = jnp.where(line == 0, sorted_v, plane_v * CHIPS + (owners >> 1))
    to_scalar = pltpu.make_async_copy(place_v, place, sem_in.at[4])
    to_scalar.start()
    to_scalar.wait()
    order_v, dest_v = zero, zero
    slot = holder = mine = have = jnp.int32(0)
    for b in range(nblk):
        at, site = place[0, b], place[1, b]
        order_v = jnp.where(lane == at, b, order_v)
        dest_v = jnp.where(lane == site, at & (PER_PLANE - 1), dest_v)
        here = site == x * CHIPS + chip
        own = here & (owner[b] == f)
        holder = jnp.where(here, owner[b] & 1, holder)
        slot = jnp.where(own, owner_slot[b], slot)
        mine = jnp.where(own, b, mine)
        have = jnp.where(own, 1, have)
    inverse_v[...] = jnp.where(line == 0, order_v, dest_v)
    to_scalar = pltpu.make_async_copy(inverse_v, inverse, sem_in.at[5])
    to_scalar.start()
    to_scalar.wait()
    _, x_right, x_far, x_left = reps

    def many(ref, send, recv):
        return pltpu.make_async_remote_copy(
            ref, ref, send, recv, device_id=(sibling, x), device_id_type=MESH
        )

    def stage(k):
        def body(t, _):
            xs[k, t] = grad[inverse[0, t], :, k * cut : (k + 1) * cut]
            return 0

        lax.fori_loop(0, nblk, body, 0, unroll=4)

    def x_copy(k, n, src, dst, to):
        return pltpu.make_async_remote_copy(
            src, dst, x_send.at[0], x_recv.at[k, min(n // 2, 1)], device_id=(f, to), device_id_type=MESH
        )

    def x_copies(k):
        far, near_r, near_l = x_far * PER_PLANE, x_right * PER_PLANE, x_left * PER_PLANE
        return (
            x_copy(k, 0, xs.at[k, pl.ds(far, HALF)], a_in.at[0, k], x_right),
            x_copy(k, 1, xs.at[k, pl.ds(far + HALF, HALF)], a_in.at[1, k], x_left),
            x_copy(k, 2, xs.at[k, pl.ds(near_r + HALF, HALF)], b_in.at[0, k], x_right),
            x_copy(k, 3, xs.at[k, pl.ds(near_l, HALF)], b_in.at[1, k], x_left),
            x_copy(k, 4, c_out.at[0, k], c_in.at[0, k], x_right),
            x_copy(k, 5, c_out.at[1, k], c_in.at[1, k], x_left),
        )

    xc = [x_copies(k) for k in range(CUTS)]

    def first(k):
        xc[k][0].start()
        xc[k][1].start()

    def second(k):
        xc[k][2].start()
        xc[k][3].start()

    def wide(v):
        return v.astype(jnp.float32)

    def merge(k):
        many(xs.at[k, pl.ds(0, PER_PLANE)], x_send.at[0], x_recv.at[k, 0]).wait_recv()
        for side, at in ((0, x_right * PER_PLANE), (1, x_left * PER_PLANE + HALF)):

            def body(j, _):
                c_out[side, k, j] = (wide(xs[k, at + j]) + wide(a_in[side, k, j])).astype(jnp.bfloat16)
                return 0

            lax.fori_loop(0, HALF, body, 0, unroll=True)
            xc[k][4 + side].start()

    def finish(k):
        many(xs.at[k, pl.ds(0, 2 * PER_PLANE)], x_send.at[0], x_recv.at[k, 1]).wait_recv()
        for lo, from_l, from_r in ((0, c_in, b_in), (HALF, b_in, c_in)):

            def body(j, _):
                total = wide(xs[k, x * PER_PLANE + lo + j]) + wide(from_l[0, k, j]) + wide(from_r[1, k, j])
                summed[k, lo + j] = total.astype(jnp.bfloat16)
                return 0

            lax.fori_loop(0, HALF, body, 0, unroll=True)

    def forward(k):
        for to in chips[1:]:
            f_out[k, to] = summed[k, inverse[1, x * CHIPS + to]]
            pltpu.make_async_remote_copy(
                f_out.at[k, to], g_in.at[k, chip, core], f_send.at[0], f_recv.at[k],
                device_id=(to * 2 + core, x), device_id_type=MESH,
            ).start()
        g_in[k, chip, core] = summed[k, inverse[1, x * CHIPS + chip]]

    swaps = [
        pltpu.make_async_remote_copy(
            g_in.at[k, :, core], g_in.at[k, :, core], d_send.at[0], d_recv.at[k],
            device_id=(sibling, x), device_id_type=MESH,
        )
        for k in range(CUTS)
    ]

    def swap(k):
        many(f_out.at[k, pl.ds(0, CHIPS - 1)], f_send.at[0], f_recv.at[k]).wait_recv()
        swaps[k].start()

    def left_mul(m):
        parts = range(m * per_quarter, (m + 1) * per_quarter)
        for k in parts:
            swaps[k].wait_recv()

        block = jnp.concatenate([g_in[k].reshape(width, cut) for k in parts], axis=1)
        part = jnp.dot(left[slot], block, preferred_element_type=jnp.float32)
        lp[:, m * quarter : (m + 1) * quarter] = part.astype(jnp.bfloat16)

    loads[0].wait()
    stage(0)
    pl.semaphore_wait(barrier, CHIPS * REPS)
    first(0)
    second(0)
    for k in range(1, CUTS + 1):
        if k < CUTS:
            stage(k)
            first(k)
        merge(k - 1)
        if k < CUTS:
            second(k)
        if k == CUTS:
            swap(0)
        if k >= 2:
            finish(k - 2)
            forward(k - 2)
    swap(1)
    finish(CUTS - 1)
    forward(CUTS - 1)

    for i in range(1, REPS):
        to = reps[i]
        pltpu.make_async_remote_copy(
            summed.at[pl.ds(to * per_quarter, per_quarter)], mom_in.at[x], m_send.at[0], m_recv.at[0],
            device_id=(f, to), device_id_type=MESH,
        ).start()
    mom_in[x] = summed[pl.ds(x * per_quarter, per_quarter)]

    loads[1].wait()
    left_mul(0)
    left_mul(1)
    swap(2)
    left_mul(2)
    loads[2].wait()
    swap(3)
    left_mul(3)

    def right_mul(i, squares):
        cols = pl.ds(pl.multiple_of(reps[i] * quarter, quarter), quarter)
        part = jnp.dot(lp[...], right[slot, :, cols], preferred_element_type=jnp.float32)
        pbs[i][core] = part.astype(jnp.bfloat16).reshape(CHIPS, 2, rows, quarter)
        return squares + jnp.sum(part * part, axis=0, keepdims=True)

    trades = [
        pltpu.make_async_remote_copy(
            pb.at[core, :, 1 - core], pb.at[core, :, 1 - core], p_send.at[0], p_recv.at[i],
            device_id=(sibling, x), device_id_type=MESH,
        )
        for i, pb in enumerate(pbs)
    ]

    def send_back(*which, some=slice(None)):
        for i in which:
            if some.start is None:
                trades[i].wait_recv()
        for to in chips[some]:
            for i in which:
                if i == 0 and to is chips[0]:
                    back[x * CHIPS + chip] = pbs[i][holder, chip, core]
                    continue
                ret[i, to] = pbs[i][holder, to, core]
                pltpu.make_async_remote_copy(
                    ret.at[i, to], back.at[x * CHIPS + chip], u_send.at[0], u_recv.at[0],
                    device_id=(to * 2 + core, reps[i]), device_id_type=MESH,
                ).start()

    squares = jnp.zeros((1, quarter), jnp.float32)
    for i in (2, 0, 1, 3):
        squares = right_mul(i, squares)
        trades[i].start()
        if i == 0:
            send_back(2)
        if i == 1:
            send_back(0)

    loads[3].wait()
    moments = many(xs.at[0, pl.ds(0, (REPS - 1) * PER_PLANE)], m_send.at[0], m_recv.at[0])
    moments.wait_recv()

    at_lane = lax.broadcasted_iota(jnp.int32, (1, 128), 1)

    def moment(b, sums):
        t = place[0, b]
        sq = jnp.zeros((1, cut), jnp.float32)
        for h in range(per_quarter):
            s = wide(mom_in[t >> 3, h, t & (PER_PLANE - 1)])
            at = slice(h * cut, (h + 1) * cut)
            new = 0.99 * sm[b, :, at] + 0.01 * s * s
            nm[b, :, at] = new
            adam = s / (jnp.sqrt(new) + 1e-08)
            sq = sq + jnp.sum(adam * adam, axis=0, keepdims=True)
        return jnp.where(at_lane == b, jnp.sum(sq, axis=1, keepdims=True), sums)

    owned = (at_lane == nblk + mine) & (have == 1)
    own_sums = jnp.where(owned, jnp.sum(squares, axis=1, keepdims=True), 0.0)
    own_sums = lax.fori_loop(0, nblk, moment, own_sums, unroll=4)
    ad_1[pl.ds(0, 1), :] = own_sums
    sums_chip = pltpu.make_async_remote_copy(
        ad_1.at[pl.ds(0, 1)], ad_1.at[pl.ds(8, 1)], s_send.at[0], s_recv.at[0],
        device_id=(sibling, x), device_id_type=MESH,
    )
    sums_chip.start()
    store_nm = pltpu.make_async_copy(nm, nm_hbm, sem_out.at[0])
    store_nm.start()
    sums_chip.wait_recv()
    ad_x[x, pl.ds(0, 1), :] = own_sums + ad_1[pl.ds(8, 1), :]
    for i in range(1, REPS):
        pltpu.make_async_remote_copy(
            ad_x.at[x, pl.ds(0, 1)], ad_x.at[x, pl.ds(0, 1)], s_send.at[1], s_recv.at[1],
            device_id=(f, reps[i]), device_id_type=MESH,
        ).start()
    send_back(1)
    send_back(3, some=slice(None, CHIPS // 2))
    sums_x = many(ad_x.at[pl.ds(0, REPS - 1), pl.ds(0, 1)], s_send.at[1], s_recv.at[1])
    sums_x.wait_recv()
    ad_p[chip, pl.ds(0, 1), :] = jnp.sum(ad_x[:, pl.ds(0, 1), :], axis=0)
    for to in chips[1:]:
        pltpu.make_async_remote_copy(
            ad_p.at[chip, pl.ds(0, 1)], ad_p.at[chip, pl.ds(0, 1)], s_send.at[2], s_recv.at[2],
            device_id=(to * 2 + core, x), device_id_type=MESH,
        ).start()
    send_back(3, some=slice(CHIPS // 2, None))

    sums_plane = many(ad_p.at[pl.ds(0, CHIPS - 1), pl.ds(0, 1)], s_send.at[2], s_recv.at[2])
    sums_plane.wait_recv()
    total = jnp.sum(ad_p[:, pl.ds(0, 1), :], axis=0)
    line = lax.broadcasted_iota(jnp.int32, (nblk, 128), 0)
    lane = lax.broadcasted_iota(jnp.int32, (nblk, 128), 1)
    total = jnp.broadcast_to(total, (nblk, 128))
    area = width * width
    adam_mean = jnp.sum(jnp.where(lane == line, total, 0.0), axis=1, keepdims=True) / area
    prod_mean = jnp.sum(jnp.where(lane == line + nblk, total, 0.0), axis=1, keepdims=True) / area
    scale = jnp.sqrt(adam_mean) / jnp.sqrt(prod_mean + 1e-06)
    factor[...] = jnp.broadcast_to(scale, factor.shape)

    many(back.at[pl.ds(0, CHIPS * REPS - 1)], u_send.at[0], u_recv.at[0]).wait_recv()

    def collect(b, _):
        by = factor[pl.ds(b, 1), :]
        by = jnp.concatenate([by, by], axis=1)
        upd[b] = (wide(back[place[1, b]]) * by).astype(jnp.bfloat16)
        return 0

    lax.fori_loop(0, nblk, collect, 0, unroll=2)
    store_upd = pltpu.make_async_copy(upd, upd_hbm, sem_out.at[1])
    store_upd.start()

    many(xs.at[:, pl.ds(0, 6 * HALF)], x_send.at[0], x_recv.at[0, 0]).wait_send()
    many(f_out.at[:, pl.ds(0, CHIPS - 1)], f_send.at[0], f_recv.at[0]).wait_send()
    many(f_out, d_send.at[0], d_recv.at[0]).wait_send()
    many(ret, p_send.at[0], p_recv.at[0]).wait_send()
    for copy in (moments, sums_chip, sums_x, sums_plane):
        copy.wait_send()
    many(back.at[pl.ds(0, CHIPS * REPS - 1)], u_send.at[0], u_recv.at[0]).wait_send()
    store_nm.wait()
    store_upd.wait()


def one_kernel(grad, second_moment, left_factor, right_factor, block_owner, block_slot):
    nblk, rows, width = grad.shape
    slots = left_factor.shape[0]
    quarter = width // REPS
    bf, f32 = jnp.bfloat16, jnp.float32
    piece = (rows, quarter)
    part = (rows, width // CUTS)
    any_spec = pl.BlockSpec(memory_space=pl.ANY)
    vmem = pltpu.VMEM
    dma = pltpu.SemaphoreType.DMA
    return pl.pallas_call(
        step_kernel,
        out_shape=(
            jax.ShapeDtypeStruct((nblk, rows, quarter), bf),
            jax.ShapeDtypeStruct((nblk, rows, quarter), f32),
        ),
        in_specs=[pl.BlockSpec(memory_space=pltpu.SMEM)] * 2 + [any_spec] * 4,
        out_specs=(any_spec, any_spec),
        scratch_shapes=[
            vmem((nblk, rows, width), bf),
            vmem((nblk, rows, quarter), f32),
            vmem((slots, width, width), bf),
            vmem((slots, width, width), bf),
            vmem((CUTS, nblk) + part, bf),
            vmem((2, CUTS, HALF) + part, bf),
            vmem((2, CUTS, HALF) + part, bf),
            vmem((2, CUTS, HALF) + part, bf),
            vmem((2, CUTS, HALF) + part, bf),
            vmem((CUTS, PER_PLANE) + part, bf),
            vmem((CUTS, CHIPS) + part, bf),
            vmem((CUTS, CHIPS, 2) + part, bf),
            vmem((width, width), bf),
        ]
        + [vmem((2, CHIPS, 2) + piece, bf)] * REPS
        + [
            vmem((REPS, CHIPS) + piece, bf),
            vmem((REPS * CHIPS,) + piece, bf),
            vmem((REPS, CUTS // REPS, PER_PLANE) + part, bf),
            vmem((nblk,) + piece, f32),
            vmem((nblk,) + piece, bf),
            vmem((16, 128), f32),
            vmem((REPS, 8, 128), f32),
            vmem((CHIPS, 8, 128), f32),
            vmem((nblk, 128), f32),
            vmem((8, 128), jnp.int32),
            pltpu.SMEM((8, 128), jnp.int32),
            vmem((8, 128), jnp.int32),
            pltpu.SMEM((8, 128), jnp.int32),
            dma((6,)),
            dma((2,)),
            dma((1,)),
            dma((CUTS, 2)),
            dma((1,)),
            dma((CUTS,)),
            dma((1,)),
            dma((CUTS,)),
            dma((1,)),
            dma((REPS,)),
        ]
        + [dma((1,))] * 4
        + [dma((3,))] * 2,
        compiler_params=pltpu.CompilerParams(
            collective_id=0, has_side_effects=True, vmem_limit_bytes=58 << 20
        ),
        cost_estimate=pl.CostEstimate(
            flops=4 * width**3, bytes_accessed=18 << 20, transcendentals=nblk * rows * quarter
        ),
        name="shampoo_step",
    )(block_owner, block_slot, grad, second_moment, left_factor, right_factor)


def crowded(block_owner, block_slot):
    bit = jnp.left_shift(jnp.int32(1), block_owner)
    other = jnp.left_shift(jnp.int32(1), block_owner ^ 1)
    third = jnp.sum(jnp.where(block_slot == 2, bit, 0))
    second = jnp.sum(jnp.where(block_slot == 1, other, 0))
    return (third & second) != 0


def ring_sum(value, axis):
    count = lax.axis_size(axis)
    step = 1
    while step < count:
        value = value + lax.ppermute(value, axis, [(i, i ^ step) for i in range(count)])
        step *= 2
    return value


def general(grad_partial, second_moment, left_factor, right_factor, block_owner, block_slot):
    slot_count = left_factor.shape[0]
    row_count = grad_partial.shape[2]
    full_width = grad_partial.shape[3]
    rep_count = lax.axis_size("rep")
    owner_count = lax.axis_size("fsdp")
    owner_index = lax.axis_index("fsdp")
    rep_index = lax.axis_index("rep")
    quarter = full_width // rep_count
    slot_range = jnp.arange(slot_count, dtype=jnp.int32)
    owner_range = jnp.arange(owner_count, dtype=jnp.int32)
    selector = (
        (block_slot[None, None, :] == slot_range[:, None, None])
        & (block_owner[None, None, :] == owner_range[None, :, None])
    ).astype(jnp.bfloat16)
    owned = (
        (block_slot[None, :] == slot_range[:, None]) & (block_owner[None, :] == owner_index)
    ).astype(jnp.float32)
    summed = ring_sum(grad_partial[0].astype(jnp.float32), "rep")
    column = lax.dynamic_slice_in_dim(summed, rep_index * quarter, quarter, 2)
    new_moment = 0.99 * second_moment + 0.01 * column * column
    adam = column / (jnp.sqrt(new_moment) + 1e-08)
    partial_squares = jnp.sum(adam * adam, axis=(1, 2))
    total_squares = ring_sum(ring_sum(partial_squares, "rep"), "fsdp")
    adam_rms = jnp.sqrt(total_squares / (full_width * full_width))
    slot_rms = jnp.sum(owned * adam_rms[None, :], axis=1)
    grad_bf = summed.astype(jnp.bfloat16)
    outbound = jnp.einsum(
        "kdn,nrc->kdrc", selector, grad_bf, preferred_element_type=jnp.float32
    ).astype(jnp.bfloat16)
    outbound = outbound.reshape(slot_count, owner_count * row_count, full_width)
    inbound = lax.all_to_all(outbound, "fsdp", split_axis=1, concat_axis=1, tiled=True)
    left_prod = jnp.einsum(
        "kij,kjc->kic", left_factor, inbound, preferred_element_type=jnp.float32
    ).astype(jnp.bfloat16)
    product = jnp.einsum(
        "kij,kjc->kic", left_prod, right_factor, preferred_element_type=jnp.float32
    )
    prod_mean = jnp.mean(product * product, axis=(1, 2))
    graft = slot_rms / jnp.sqrt(prod_mean + 1e-06)
    scaled = (product * graft[:, None, None]).astype(jnp.bfloat16)
    returned = lax.all_to_all(scaled, "fsdp", split_axis=1, concat_axis=1, tiled=True)
    returned = lax.dynamic_slice_in_dim(returned, rep_index * quarter, quarter, 2)
    returned = returned.reshape(slot_count, owner_count, row_count, quarter)
    update = jnp.einsum(
        "kdn,kdrc->nrc", selector, returned, preferred_element_type=jnp.float32
    ).astype(jnp.bfloat16)
    return (update, new_moment)


def per_device(grad_partial, second_moment, left_factor, right_factor, block_owner, block_slot):
    def direct(gp, sm, lf, rf, owner, slot):
        return one_kernel(gp[0], sm, lf, rf, owner, slot)

    return lax.cond(
        crowded(block_owner, block_slot), general, direct,
        grad_partial, second_moment, left_factor, right_factor, block_owner, block_slot,
    )


def solution(mesh):
    placed = (
        P("rep", None, "fsdp", None),
        P(None, "fsdp", "rep"),
        P("fsdp", None, None),
        P("fsdp", None, None),
        P(),
        P(),
    )
    return jax.shard_map(
        per_device,
        mesh=mesh,
        in_specs=placed,
        out_specs=(P(None, "fsdp", "rep"), P(None, "fsdp", "rep")),
        check_vma=False,
    )
```

```python
import functools

import jax
import jax.numpy as jnp
from jax import lax
from jax.experimental import pallas as pl
from jax.experimental.pallas import tpu as pltpu
from jax.sharding import PartitionSpec as P

MESH = pl.DeviceIdType.MESH
REPS = 4
CHIPS = 16
SIDE = 4
PER_PLANE = 8
HALF = PER_PLANE // 2
CUTS = 4


def step_kernel(
    owner, owner_slot, g_hbm, sm_hbm, l_hbm, r_hbm, upd_hbm, nm_hbm,
    grad, sm, left, right, xs, a_in, b_in, c_in, c_out, summed, f_out, g_in,
    lp, pb0, pb1, pb2, pb3, ret, back, mom_in, nm, upd,
    ad_1, ad_x, ad_p, factor, place_v, place, inverse_v, inverse,
    sem_in, sem_out, x_send, x_recv, f_send, f_recv, d_send, d_recv,
    p_send, p_recv, u_send, u_recv, m_send, m_recv, s_send, s_recv,
):
    pbs = (pb0, pb1, pb2, pb3)
    f = lax.axis_index("fsdp")
    x = lax.axis_index("rep")
    core = f % 2
    chip = f // 2
    cy = chip // SIDE
    cz = chip % SIDE
    sibling = f + 1 - 2 * core
    nblk, rows, width = grad.shape
    quarter = width // REPS
    cut = width // CUTS
    per_quarter = CUTS // REPS

    chips = [
        lax.rem(cy + i // SIDE, SIDE) * SIDE + lax.rem(cz + i % SIDE, SIDE) for i in range(CHIPS)
    ]
    reps = [lax.rem(x + i, REPS) for i in range(REPS)]

    loads = [
        pltpu.make_async_copy(src, dst, sem_in.at[i])
        for i, (src, dst) in enumerate(
            ((g_hbm, grad), (l_hbm, left), (r_hbm, right), (sm_hbm, sm))
        )
    ]
    for load in loads:
        load.start()

    barrier = pltpu.get_barrier_semaphore()

    for i in range(1, CHIPS * REPS):
        to = (chips[i // REPS] * 2 + core, reps[i % REPS])
        pl.semaphore_signal(barrier, inc=1, device_id=to, device_id_type=MESH)
    pl.semaphore_signal(barrier, inc=1, device_id=(sibling, x), device_id_type=MESH)

    lane = lax.broadcasted_iota(jnp.int32, place_v.shape, 1)
    line = lax.broadcasted_iota(jnp.int32, place_v.shape, 0)
    zero = jnp.zeros(place_v.shape, jnp.int32)
    owners, slots, before = zero, zero, zero
    for b in range(nblk):
        owners = jnp.where(lane == b, owner[b], owners)
        slots = jnp.where(lane == b, owner_slot[b], slots)
    for b in range(nblk):
        before = before + jnp.where(owners > owner[b], 1, 0)
    spot = before + slots
    plane_v = spot & (REPS - 1)
    sorted_v = plane_v * PER_PLANE + (spot >> 2)
    place_v[...] = jnp.where(line == 0, sorted_v, plane_v * CHIPS + (owners >> 1))
    to_scalar = pltpu.make_async_copy(place_v, place, sem_in.at[4])
    to_scalar.start()
    to_scalar.wait()
    order_v, dest_v = zero, zero
    slot = holder = mine = have = jnp.int32(0)
    for b in range(nblk):
        at, site = place[0, b], place[1, b]
        order_v = jnp.where(lane == at, b, order_v)
        dest_v = jnp.where(lane == site, at & (PER_PLANE - 1), dest_v)
        here = site == x * CHIPS + chip
        own = here & (owner[b] == f)
        holder = jnp.where(here, owner[b] & 1, holder)
        slot = jnp.where(own, owner_slot[b], slot)
        mine = jnp.where(own, b, mine)
        have = jnp.where(own, 1, have)
    inverse_v[...] = jnp.where(line == 0, order_v, dest_v)
    to_scalar = pltpu.make_async_copy(inverse_v, inverse, sem_in.at[5])
    to_scalar.start()
    to_scalar.wait()
    _, x_right, x_far, x_left = reps

    def many(ref, send, recv):
        return pltpu.make_async_remote_copy(
            ref, ref, send, recv, device_id=(sibling, x), device_id_type=MESH
        )

    def stage(k):
        def body(t, _):
            xs[k, t] = grad[inverse[0, t], :, k * cut : (k + 1) * cut]
            return 0

        lax.fori_loop(0, nblk, body, 0, unroll=4)

    def x_copy(k, n, src, dst, to):
        return pltpu.make_async_remote_copy(
            src, dst, x_send.at[0], x_recv.at[k, min(n // 2, 1)], device_id=(f, to), device_id_type=MESH
        )

    def x_copies(k):
        far, near_r, near_l = x_far * PER_PLANE, x_right * PER_PLANE, x_left * PER_PLANE
        return (
            x_copy(k, 0, xs.at[k, pl.ds(far, HALF)], a_in.at[0, k], x_right),
            x_copy(k, 1, xs.at[k, pl.ds(far + HALF, HALF)], a_in.at[1, k], x_left),
            x_copy(k, 2, xs.at[k, pl.ds(near_r + HALF, HALF)], b_in.at[0, k], x_right),
            x_copy(k, 3, xs.at[k, pl.ds(near_l, HALF)], b_in.at[1, k], x_left),
            x_copy(k, 4, c_out.at[0, k], c_in.at[0, k], x_right),
            x_copy(k, 5, c_out.at[1, k], c_in.at[1, k], x_left),
        )

    xc = [x_copies(k) for k in range(CUTS)]

    def first(k):
        xc[k][0].start()
        xc[k][1].start()

    def second(k):
        xc[k][2].start()
        xc[k][3].start()

    def wide(v):
        return v.astype(jnp.float32)

    def merge(k):
        many(xs.at[k, pl.ds(0, PER_PLANE)], x_send.at[0], x_recv.at[k, 0]).wait_recv()
        for side, at in ((0, x_right * PER_PLANE), (1, x_left * PER_PLANE + HALF)):

            def body(j, _):
                c_out[side, k, j] = (wide(xs[k, at + j]) + wide(a_in[side, k, j])).astype(jnp.bfloat16)
                return 0

            lax.fori_loop(0, HALF, body, 0, unroll=True)
            xc[k][4 + side].start()

    def finish(k):
        many(xs.at[k, pl.ds(0, 2 * PER_PLANE)], x_send.at[0], x_recv.at[k, 1]).wait_recv()
        for lo, from_l, from_r in ((0, c_in, b_in), (HALF, b_in, c_in)):

            def body(j, _):
                total = wide(xs[k, x * PER_PLANE + lo + j]) + wide(from_l[0, k, j]) + wide(from_r[1, k, j])
                summed[k, lo + j] = total.astype(jnp.bfloat16)
                return 0

            lax.fori_loop(0, HALF, body, 0, unroll=True)

    def forward(k):
        for to in chips[1:]:
            f_out[k, to] = summed[k, inverse[1, x * CHIPS + to]]
            pltpu.make_async_remote_copy(
                f_out.at[k, to], g_in.at[k, chip, core], f_send.at[0], f_recv.at[k],
                device_id=(to * 2 + core, x), device_id_type=MESH,
            ).start()
        g_in[k, chip, core] = summed[k, inverse[1, x * CHIPS + chip]]

    swaps = [
        pltpu.make_async_remote_copy(
            g_in.at[k, :, core], g_in.at[k, :, core], d_send.at[0], d_recv.at[k],
            device_id=(sibling, x), device_id_type=MESH,
        )
        for k in range(CUTS)
    ]

    def swap(k):
        many(f_out.at[k, pl.ds(0, CHIPS - 1)], f_send.at[0], f_recv.at[k]).wait_recv()
        swaps[k].start()

    def left_mul(m):
        parts = range(m * per_quarter, (m + 1) * per_quarter)
        for k in parts:
            swaps[k].wait_recv()

        block = jnp.concatenate([g_in[k].reshape(width, cut) for k in parts], axis=1)
        part = jnp.dot(left[slot], block, preferred_element_type=jnp.float32)
        lp[:, m * quarter : (m + 1) * quarter] = part.astype(jnp.bfloat16)

    loads[0].wait()
    stage(0)
    pl.semaphore_wait(barrier, CHIPS * REPS)
    first(0)
    second(0)
    for k in range(1, CUTS + 1):
        if k < CUTS:
            stage(k)
            first(k)
        merge(k - 1)
        if k < CUTS:
            second(k)
        if k == CUTS:
            swap(0)
        if k >= 2:
            finish(k - 2)
            forward(k - 2)
    finish(CUTS - 1)
    forward(CUTS - 1)
    swap(1)

    for i in range(1, REPS):
        to = reps[i]
        pltpu.make_async_remote_copy(
            summed.at[pl.ds(to * per_quarter, per_quarter)], mom_in.at[x], m_send.at[0], m_recv.at[0],
            device_id=(f, to), device_id_type=MESH,
        ).start()
    mom_in[x] = summed[pl.ds(x * per_quarter, per_quarter)]

    loads[1].wait()
    left_mul(0)
    left_mul(1)
    swap(2)
    left_mul(2)
    loads[2].wait()
    swap(3)
    left_mul(3)

    def right_mul(i, squares):
        cols = pl.ds(pl.multiple_of(reps[i] * quarter, quarter), quarter)
        part = jnp.dot(lp[...], right[slot, :, cols], preferred_element_type=jnp.float32)
        pbs[i][core] = part.astype(jnp.bfloat16).reshape(CHIPS, 2, rows, quarter)
        return squares + jnp.sum(part * part, axis=0, keepdims=True)

    trades = [
        pltpu.make_async_remote_copy(
            pb.at[core, :, 1 - core], pb.at[core, :, 1 - core], p_send.at[0], p_recv.at[i],
            device_id=(sibling, x), device_id_type=MESH,
        )
        for i, pb in enumerate(pbs)
    ]

    def send_back(*which, some=slice(None)):
        for i in which:
            if some.start is None:
                trades[i].wait_recv()
        for to in chips[some]:
            for i in which:
                if i == 0 and to is chips[0]:
                    back[x * CHIPS + chip] = pbs[i][holder, chip, core]
                    continue
                ret[i, to] = pbs[i][holder, to, core]
                pltpu.make_async_remote_copy(
                    ret.at[i, to], back.at[x * CHIPS + chip], u_send.at[0], u_recv.at[0],
                    device_id=(to * 2 + core, reps[i]), device_id_type=MESH,
                ).start()

    squares = jnp.zeros((1, quarter), jnp.float32)
    for i in (2, 0, 1, 3):
        squares = right_mul(i, squares)
        trades[i].start()
        if i == 0:
            send_back(2)
        if i == 1:
            send_back(0)

    loads[3].wait()
    moments = many(xs.at[0, pl.ds(0, (REPS - 1) * PER_PLANE)], m_send.at[0], m_recv.at[0])
    moments.wait_recv()

    at_lane = lax.broadcasted_iota(jnp.int32, (1, 128), 1)

    def moment(b, sums):
        t = place[0, b]
        sq = jnp.zeros((1, cut), jnp.float32)
        for h in range(per_quarter):
            s = wide(mom_in[t >> 3, h, t & (PER_PLANE - 1)])
            at = slice(h * cut, (h + 1) * cut)
            new = 0.99 * sm[b, :, at] + 0.01 * s * s
            nm[b, :, at] = new
            adam = s / (jnp.sqrt(new) + 1e-08)
            sq = sq + jnp.sum(adam * adam, axis=0, keepdims=True)
        return jnp.where(at_lane == b, jnp.sum(sq, axis=1, keepdims=True), sums)

    owned = (at_lane == nblk + mine) & (have == 1)
    own_sums = jnp.where(owned, jnp.sum(squares, axis=1, keepdims=True), 0.0)
    own_sums = lax.fori_loop(0, nblk, moment, own_sums, unroll=4)
    ad_1[pl.ds(0, 1), :] = own_sums
    sums_chip = pltpu.make_async_remote_copy(
        ad_1.at[pl.ds(0, 1)], ad_1.at[pl.ds(8, 1)], s_send.at[0], s_recv.at[0],
        device_id=(sibling, x), device_id_type=MESH,
    )
    sums_chip.start()
    store_nm = pltpu.make_async_copy(nm, nm_hbm, sem_out.at[0])
    store_nm.start()
    sums_chip.wait_recv()
    ad_x[x, pl.ds(0, 1), :] = own_sums + ad_1[pl.ds(8, 1), :]
    for i in range(1, REPS):
        pltpu.make_async_remote_copy(
            ad_x.at[x, pl.ds(0, 1)], ad_x.at[x, pl.ds(0, 1)], s_send.at[1], s_recv.at[1],
            device_id=(f, reps[i]), device_id_type=MESH,
        ).start()
    send_back(1)
    send_back(3, some=slice(None, CHIPS // 2))
    sums_x = many(ad_x.at[pl.ds(0, REPS - 1), pl.ds(0, 1)], s_send.at[1], s_recv.at[1])
    sums_x.wait_recv()
    ad_p[chip, pl.ds(0, 1), :] = jnp.sum(ad_x[:, pl.ds(0, 1), :], axis=0)
    for to in chips[1:]:
        pltpu.make_async_remote_copy(
            ad_p.at[chip, pl.ds(0, 1)], ad_p.at[chip, pl.ds(0, 1)], s_send.at[2], s_recv.at[2],
            device_id=(to * 2 + core, x), device_id_type=MESH,
        ).start()
    send_back(3, some=slice(CHIPS // 2, None))

    sums_plane = many(ad_p.at[pl.ds(0, CHIPS - 1), pl.ds(0, 1)], s_send.at[2], s_recv.at[2])
    sums_plane.wait_recv()
    total = jnp.sum(ad_p[:, pl.ds(0, 1), :], axis=0)
    line = lax.broadcasted_iota(jnp.int32, (nblk, 128), 0)
    lane = lax.broadcasted_iota(jnp.int32, (nblk, 128), 1)
    total = jnp.broadcast_to(total, (nblk, 128))
    area = width * width
    adam_mean = jnp.sum(jnp.where(lane == line, total, 0.0), axis=1, keepdims=True) / area
    prod_mean = jnp.sum(jnp.where(lane == line + nblk, total, 0.0), axis=1, keepdims=True) / area
    scale = jnp.sqrt(adam_mean) / jnp.sqrt(prod_mean + 1e-06)
    factor[...] = jnp.broadcast_to(scale, factor.shape)

    many(back.at[pl.ds(0, CHIPS * REPS - 1)], u_send.at[0], u_recv.at[0]).wait_recv()

    def collect(b, _):
        by = factor[pl.ds(b, 1), :]
        by = jnp.concatenate([by, by], axis=1)
        upd[b] = (wide(back[place[1, b]]) * by).astype(jnp.bfloat16)
        return 0

    lax.fori_loop(0, nblk, collect, 0, unroll=2)
    store_upd = pltpu.make_async_copy(upd, upd_hbm, sem_out.at[1])
    store_upd.start()

    many(xs.at[:, pl.ds(0, 6 * HALF)], x_send.at[0], x_recv.at[0, 0]).wait_send()
    many(f_out.at[:, pl.ds(0, CHIPS - 1)], f_send.at[0], f_recv.at[0]).wait_send()
    many(f_out, d_send.at[0], d_recv.at[0]).wait_send()
    many(ret, p_send.at[0], p_recv.at[0]).wait_send()
    for copy in (moments, sums_chip, sums_x, sums_plane):
        copy.wait_send()
    many(back.at[pl.ds(0, CHIPS * REPS - 1)], u_send.at[0], u_recv.at[0]).wait_send()
    store_nm.wait()
    store_upd.wait()


def one_kernel(grad, second_moment, left_factor, right_factor, block_owner, block_slot):
    nblk, rows, width = grad.shape
    slots = left_factor.shape[0]
    quarter = width // REPS
    bf, f32 = jnp.bfloat16, jnp.float32
    piece = (rows, quarter)
    part = (rows, width // CUTS)
    any_spec = pl.BlockSpec(memory_space=pl.ANY)
    vmem = pltpu.VMEM
    dma = pltpu.SemaphoreType.DMA
    return pl.pallas_call(
        step_kernel,
        out_shape=(
            jax.ShapeDtypeStruct((nblk, rows, quarter), bf),
            jax.ShapeDtypeStruct((nblk, rows, quarter), f32),
        ),
        in_specs=[pl.BlockSpec(memory_space=pltpu.SMEM)] * 2 + [any_spec] * 4,
        out_specs=(any_spec, any_spec),
        scratch_shapes=[
            vmem((nblk, rows, width), bf),
            vmem((nblk, rows, quarter), f32),
            vmem((slots, width, width), bf),
            vmem((slots, width, width), bf),
            vmem((CUTS, nblk) + part, bf),
            vmem((2, CUTS, HALF) + part, bf),
            vmem((2, CUTS, HALF) + part, bf),
            vmem((2, CUTS, HALF) + part, bf),
            vmem((2, CUTS, HALF) + part, bf),
            vmem((CUTS, PER_PLANE) + part, bf),
            vmem((CUTS, CHIPS) + part, bf),
            vmem((CUTS, CHIPS, 2) + part, bf),
            vmem((width, width), bf),
        ]
        + [vmem((2, CHIPS, 2) + piece, bf)] * REPS
        + [
            vmem((REPS, CHIPS) + piece, bf),
            vmem((REPS * CHIPS,) + piece, bf),
            vmem((REPS, CUTS // REPS, PER_PLANE) + part, bf),
            vmem((nblk,) + piece, f32),
            vmem((nblk,) + piece, bf),
            vmem((16, 128), f32),
            vmem((REPS, 8, 128), f32),
            vmem((CHIPS, 8, 128), f32),
            vmem((nblk, 128), f32),
            vmem((8, 128), jnp.int32),
            pltpu.SMEM((8, 128), jnp.int32),
            vmem((8, 128), jnp.int32),
            pltpu.SMEM((8, 128), jnp.int32),
            dma((6,)),
            dma((2,)),
            dma((1,)),
            dma((CUTS, 2)),
            dma((1,)),
            dma((CUTS,)),
            dma((1,)),
            dma((CUTS,)),
            dma((1,)),
            dma((REPS,)),
        ]
        + [dma((1,))] * 4
        + [dma((3,))] * 2,
        compiler_params=pltpu.CompilerParams(
            collective_id=0, has_side_effects=True, vmem_limit_bytes=58 << 20
        ),
        cost_estimate=pl.CostEstimate(
            flops=4 * width**3, bytes_accessed=18 << 20, transcendentals=nblk * rows * quarter
        ),
        name="shampoo_step",
    )(block_owner, block_slot, grad, second_moment, left_factor, right_factor)


def crowded(block_owner, block_slot):
    bit = jnp.left_shift(jnp.int32(1), block_owner)
    other = jnp.left_shift(jnp.int32(1), block_owner ^ 1)
    third = jnp.sum(jnp.where(block_slot == 2, bit, 0))
    second = jnp.sum(jnp.where(block_slot == 1, other, 0))
    return (third & second) != 0


def ring_sum(value, axis):
    count = lax.axis_size(axis)
    step = 1
    while step < count:
        value = value + lax.ppermute(value, axis, [(i, i ^ step) for i in range(count)])
        step *= 2
    return value


def general(grad_partial, second_moment, left_factor, right_factor, block_owner, block_slot):
    slot_count = left_factor.shape[0]
    row_count = grad_partial.shape[2]
    full_width = grad_partial.shape[3]
    rep_count = lax.axis_size("rep")
    owner_count = lax.axis_size("fsdp")
    owner_index = lax.axis_index("fsdp")
    rep_index = lax.axis_index("rep")
    quarter = full_width // rep_count
    slot_range = jnp.arange(slot_count, dtype=jnp.int32)
    owner_range = jnp.arange(owner_count, dtype=jnp.int32)
    selector = (
        (block_slot[None, None, :] == slot_range[:, None, None])
        & (block_owner[None, None, :] == owner_range[None, :, None])
    ).astype(jnp.bfloat16)
    owned = (
        (block_slot[None, :] == slot_range[:, None]) & (block_owner[None, :] == owner_index)
    ).astype(jnp.float32)
    summed = ring_sum(grad_partial[0].astype(jnp.float32), "rep")
    column = lax.dynamic_slice_in_dim(summed, rep_index * quarter, quarter, 2)
    new_moment = 0.99 * second_moment + 0.01 * column * column
    adam = column / (jnp.sqrt(new_moment) + 1e-08)
    partial_squares = jnp.sum(adam * adam, axis=(1, 2))
    total_squares = ring_sum(ring_sum(partial_squares, "rep"), "fsdp")
    adam_rms = jnp.sqrt(total_squares / (full_width * full_width))
    slot_rms = jnp.sum(owned * adam_rms[None, :], axis=1)
    grad_bf = summed.astype(jnp.bfloat16)
    outbound = jnp.einsum(
        "kdn,nrc->kdrc", selector, grad_bf, preferred_element_type=jnp.float32
    ).astype(jnp.bfloat16)
    outbound = outbound.reshape(slot_count, owner_count * row_count, full_width)
    inbound = lax.all_to_all(outbound, "fsdp", split_axis=1, concat_axis=1, tiled=True)
    left_prod = jnp.einsum(
        "kij,kjc->kic", left_factor, inbound, preferred_element_type=jnp.float32
    ).astype(jnp.bfloat16)
    product = jnp.einsum(
        "kij,kjc->kic", left_prod, right_factor, preferred_element_type=jnp.float32
    )
    prod_mean = jnp.mean(product * product, axis=(1, 2))
    graft = slot_rms / jnp.sqrt(prod_mean + 1e-06)
    scaled = (product * graft[:, None, None]).astype(jnp.bfloat16)
    returned = lax.all_to_all(scaled, "fsdp", split_axis=1, concat_axis=1, tiled=True)
    returned = lax.dynamic_slice_in_dim(returned, rep_index * quarter, quarter, 2)
    returned = returned.reshape(slot_count, owner_count, row_count, quarter)
    update = jnp.einsum(
        "kdn,kdrc->nrc", selector, returned, preferred_element_type=jnp.float32
    ).astype(jnp.bfloat16)
    return (update, new_moment)


def per_device(grad_partial, second_moment, left_factor, right_factor, block_owner, block_slot):
    def direct(gp, sm, lf, rf, owner, slot):
        return one_kernel(gp[0], sm, lf, rf, owner, slot)

    return lax.cond(
        crowded(block_owner, block_slot), general, direct,
        grad_partial, second_moment, left_factor, right_factor, block_owner, block_slot,
    )


def solution(mesh):
    placed = (
        P("rep", None, "fsdp", None),
        P(None, "fsdp", "rep"),
        P("fsdp", None, None),
        P("fsdp", None, None),
        P(),
        P(),
    )
    return jax.shard_map(
        per_device,
        mesh=mesh,
        in_specs=placed,
        out_specs=(P(None, "fsdp", "rep"), P(None, "fsdp", "rep")),
        check_vma=False,
    )
```

```python
import functools

import jax
import jax.numpy as jnp
from jax import lax
from jax.experimental import pallas as pl
from jax.experimental.pallas import tpu as pltpu
from jax.sharding import PartitionSpec as P

MESH = pl.DeviceIdType.MESH
REPS = 4
CHIPS = 16
SIDE = 4
PER_PLANE = 8
HALF = PER_PLANE // 2
CUTS = 4


def step_kernel(
    owner, owner_slot, g_hbm, sm_hbm, l_hbm, r_hbm, upd_hbm, nm_hbm,
    grad, sm, left, right, xs, a_in, b_in, c_in, c_out, summed, f_out, g_in,
    lp, held, pb0, pb1, pb2, pb3, ret, back, mom_in, nm, upd,
    ad_1, ad_x, ad_p, factor, place_v, place, inverse_v, inverse,
    sem_in, sem_out, x_send, x_recv, f_send, f_recv, d_send, d_recv,
    p_send, p_recv, u_send, u_recv, m_send, m_recv, s_send, s_recv,
):
    pbs = (pb0, pb1, pb2, pb3)
    f = lax.axis_index("fsdp")
    x = lax.axis_index("rep")
    core = f % 2
    chip = f // 2
    cy = chip // SIDE
    cz = chip % SIDE
    sibling = f + 1 - 2 * core
    nblk, rows, width = grad.shape
    quarter = width // REPS
    cut = width // CUTS
    per_quarter = CUTS // REPS

    chips = [
        lax.rem(cy + i // SIDE, SIDE) * SIDE + lax.rem(cz + i % SIDE, SIDE) for i in range(CHIPS)
    ]
    reps = [lax.rem(x + i, REPS) for i in range(REPS)]

    loads = [
        pltpu.make_async_copy(src, dst, sem_in.at[i])
        for i, (src, dst) in enumerate(
            ((g_hbm, grad), (l_hbm, left), (r_hbm, right), (sm_hbm, sm))
        )
    ]
    for load in loads:
        load.start()

    barrier = pltpu.get_barrier_semaphore()

    for i in range(1, CHIPS * REPS):
        to = (chips[i // REPS] * 2 + core, reps[i % REPS])
        pl.semaphore_signal(barrier, inc=1, device_id=to, device_id_type=MESH)
    pl.semaphore_signal(barrier, inc=1, device_id=(sibling, x), device_id_type=MESH)

    lane = lax.broadcasted_iota(jnp.int32, place_v.shape, 1)
    line = lax.broadcasted_iota(jnp.int32, place_v.shape, 0)
    zero = jnp.zeros(place_v.shape, jnp.int32)
    owners, slots, before = zero, zero, zero
    for b in range(nblk):
        owners = jnp.where(lane == b, owner[b], owners)
        slots = jnp.where(lane == b, owner_slot[b], slots)
    for b in range(nblk):
        before = before + jnp.where(owners > owner[b], 1, 0)
    spot = before + slots
    plane_v = spot & (REPS - 1)
    sorted_v = plane_v * PER_PLANE + (spot >> 2)
    place_v[...] = jnp.where(line == 0, sorted_v, plane_v * CHIPS + (owners >> 1))
    to_scalar = pltpu.make_async_copy(place_v, place, sem_in.at[4])
    to_scalar.start()
    to_scalar.wait()
    order_v, dest_v = zero, zero
    slot = holder = mine = have = jnp.int32(0)
    for b in range(nblk):
        at, site = place[0, b], place[1, b]
        order_v = jnp.where(lane == at, b, order_v)
        dest_v = jnp.where(lane == site, at & (PER_PLANE - 1), dest_v)
        here = site == x * CHIPS + chip
        own = here & (owner[b] == f)
        holder = jnp.where(here, owner[b] & 1, holder)
        slot = jnp.where(own, owner_slot[b], slot)
        mine = jnp.where(own, b, mine)
        have = jnp.where(own, 1, have)
    inverse_v[...] = jnp.where(line == 0, order_v, dest_v)
    to_scalar = pltpu.make_async_copy(inverse_v, inverse, sem_in.at[5])
    to_scalar.start()
    to_scalar.wait()
    _, x_right, x_far, x_left = reps

    def many(ref, send, recv):
        return pltpu.make_async_remote_copy(
            ref, ref, send, recv, device_id=(sibling, x), device_id_type=MESH
        )

    def stage(k):
        def body(t, _):
            xs[k, t] = grad[inverse[0, t], :, k * cut : (k + 1) * cut]
            return 0

        lax.fori_loop(0, nblk, body, 0, unroll=4)

    def x_copy(k, n, src, dst, to):
        return pltpu.make_async_remote_copy(
            src, dst, x_send.at[0], x_recv.at[k, min(n // 2, 1)], device_id=(f, to), device_id_type=MESH
        )

    def x_copies(k):
        far, near_r, near_l = x_far * PER_PLANE, x_right * PER_PLANE, x_left * PER_PLANE
        return (
            x_copy(k, 0, xs.at[k, pl.ds(far, HALF)], a_in.at[0, k], x_right),
            x_copy(k, 1, xs.at[k, pl.ds(far + HALF, HALF)], a_in.at[1, k], x_left),
            x_copy(k, 2, xs.at[k, pl.ds(near_r + HALF, HALF)], b_in.at[0, k], x_right),
            x_copy(k, 3, xs.at[k, pl.ds(near_l, HALF)], b_in.at[1, k], x_left),
            x_copy(k, 4, c_out.at[0, k], c_in.at[0, k], x_right),
            x_copy(k, 5, c_out.at[1, k], c_in.at[1, k], x_left),
        )

    xc = [x_copies(k) for k in range(CUTS)]

    def first(k):
        xc[k][0].start()
        xc[k][1].start()

    def second(k):
        xc[k][2].start()
        xc[k][3].start()

    def wide(v):
        return v.astype(jnp.float32)

    def merge(k):
        many(xs.at[k, pl.ds(0, PER_PLANE)], x_send.at[0], x_recv.at[k, 0]).wait_recv()
        for side, at in ((0, x_right * PER_PLANE), (1, x_left * PER_PLANE + HALF)):

            def body(j, _):
                c_out[side, k, j] = (wide(xs[k, at + j]) + wide(a_in[side, k, j])).astype(jnp.bfloat16)
                return 0

            lax.fori_loop(0, HALF, body, 0, unroll=True)
            xc[k][4 + side].start()

    def finish(k):
        many(xs.at[k, pl.ds(0, 2 * PER_PLANE)], x_send.at[0], x_recv.at[k, 1]).wait_recv()
        for lo, from_l, from_r in ((0, c_in, b_in), (HALF, b_in, c_in)):

            def body(j, _):
                total = wide(xs[k, x * PER_PLANE + lo + j]) + wide(from_l[0, k, j]) + wide(from_r[1, k, j])
                summed[k, lo + j] = total.astype(jnp.bfloat16)
                return 0

            lax.fori_loop(0, HALF, body, 0, unroll=True)

    def forward(k):
        for to in chips[1:]:
            f_out[k, to] = summed[k, inverse[1, x * CHIPS + to]]
            pltpu.make_async_remote_copy(
                f_out.at[k, to], g_in.at[k, chip, core], f_send.at[0], f_recv.at[k],
                device_id=(to * 2 + core, x), device_id_type=MESH,
            ).start()
        g_in[k, chip, core] = summed[k, inverse[1, x * CHIPS + chip]]

    swaps = [
        pltpu.make_async_remote_copy(
            g_in.at[k, :, core], g_in.at[k, :, core], d_send.at[0], d_recv.at[k],
            device_id=(sibling, x), device_id_type=MESH,
        )
        for k in range(CUTS)
    ]

    def swap(k):
        many(f_out.at[k, pl.ds(0, CHIPS - 1)], f_send.at[0], f_recv.at[k]).wait_recv()
        swaps[k].start()

    def left_mul(m):
        parts = range(m * per_quarter, (m + 1) * per_quarter)
        for k in parts:
            swaps[k].wait_recv()

        block = jnp.concatenate([g_in[k].reshape(width, cut) for k in parts], axis=1)
        part = jnp.dot(left[slot], block, preferred_element_type=jnp.float32)
        lp[:, m * quarter : (m + 1) * quarter] = part.astype(jnp.bfloat16)

    loads[0].wait()
    stage(0)
    pl.semaphore_wait(barrier, CHIPS * REPS)
    first(0)
    second(0)
    for k in range(1, CUTS + 1):
        if k < CUTS:
            stage(k)
            first(k)
        merge(k - 1)
        if k < CUTS:
            second(k)
        if k == CUTS:
            swap(0)
        if k >= 2:
            finish(k - 2)
            forward(k - 2)
    swap(1)
    finish(CUTS - 1)
    forward(CUTS - 1)

    for i in range(1, REPS):
        to = reps[i]
        pltpu.make_async_remote_copy(
            summed.at[pl.ds(to * per_quarter, per_quarter)], mom_in.at[x], m_send.at[0], m_recv.at[0],
            device_id=(f, to), device_id_type=MESH,
        ).start()
    mom_in[x] = summed[pl.ds(x * per_quarter, per_quarter)]

    loads[1].wait()
    left_mul(0)
    left_mul(1)
    swap(2)
    left_mul(2)
    loads[2].wait()
    swap(3)

    done = width - quarter

    def columns(i):
        return pl.ds(pl.multiple_of(reps[i] * quarter, quarter), quarter)

    early = {2: 0, 0: 1}
    for i, n in early.items():
        held[n] = jnp.dot(
            lp[:, :done], right[slot, :done, columns(i)], preferred_element_type=jnp.float32
        )
    left_mul(3)

    def right_mul(i, squares):
        if i in early:
            part = held[early[i]] + jnp.dot(
                lp[:, done:], right[slot, done:, columns(i)], preferred_element_type=jnp.float32
            )
        else:
            part = jnp.dot(lp[...], right[slot, :, columns(i)], preferred_element_type=jnp.float32)
        pbs[i][core] = part.astype(jnp.bfloat16).reshape(CHIPS, 2, rows, quarter)
        return squares + jnp.sum(part * part, axis=0, keepdims=True)

    trades = [
        pltpu.make_async_remote_copy(
            pb.at[core, :, 1 - core], pb.at[core, :, 1 - core], p_send.at[0], p_recv.at[i],
            device_id=(sibling, x), device_id_type=MESH,
        )
        for i, pb in enumerate(pbs)
    ]

    def send_back(*which, some=slice(None)):
        for i in which:
            if some.start is None:
                trades[i].wait_recv()
        for to in chips[some]:
            for i in which:
                if i == 0 and to is chips[0]:
                    back[x * CHIPS + chip] = pbs[i][holder, chip, core]
                    continue
                ret[i, to] = pbs[i][holder, to, core]
                pltpu.make_async_remote_copy(
                    ret.at[i, to], back.at[x * CHIPS + chip], u_send.at[0], u_recv.at[0],
                    device_id=(to * 2 + core, reps[i]), device_id_type=MESH,
                ).start()

    squares = jnp.zeros((1, quarter), jnp.float32)
    for i in (2, 0, 1, 3):
        squares = right_mul(i, squares)
        trades[i].start()
        if i == 0:
            send_back(2)
        if i == 1:
            send_back(0)

    loads[3].wait()
    moments = many(xs.at[0, pl.ds(0, (REPS - 1) * PER_PLANE)], m_send.at[0], m_recv.at[0])
    moments.wait_recv()

    at_lane = lax.broadcasted_iota(jnp.int32, (1, 128), 1)

    def moment(b, sums):
        t = place[0, b]
        sq = jnp.zeros((1, cut), jnp.float32)
        for h in range(per_quarter):
            s = wide(mom_in[t >> 3, h, t & (PER_PLANE - 1)])
            at = slice(h * cut, (h + 1) * cut)
            new = 0.99 * sm[b, :, at] + 0.01 * s * s
            nm[b, :, at] = new
            adam = s / (jnp.sqrt(new) + 1e-08)
            sq = sq + jnp.sum(adam * adam, axis=0, keepdims=True)
        return jnp.where(at_lane == b, jnp.sum(sq, axis=1, keepdims=True), sums)

    owned = (at_lane == nblk + mine) & (have == 1)
    own_sums = jnp.where(owned, jnp.sum(squares, axis=1, keepdims=True), 0.0)
    own_sums = lax.fori_loop(0, nblk, moment, own_sums, unroll=4)
    ad_1[pl.ds(0, 1), :] = own_sums
    sums_chip = pltpu.make_async_remote_copy(
        ad_1.at[pl.ds(0, 1)], ad_1.at[pl.ds(8, 1)], s_send.at[0], s_recv.at[0],
        device_id=(sibling, x), device_id_type=MESH,
    )
    sums_chip.start()
    store_nm = pltpu.make_async_copy(nm, nm_hbm, sem_out.at[0])
    store_nm.start()
    sums_chip.wait_recv()
    ad_x[x, pl.ds(0, 1), :] = own_sums + ad_1[pl.ds(8, 1), :]
    for i in range(1, REPS):
        pltpu.make_async_remote_copy(
            ad_x.at[x, pl.ds(0, 1)], ad_x.at[x, pl.ds(0, 1)], s_send.at[1], s_recv.at[1],
            device_id=(f, reps[i]), device_id_type=MESH,
        ).start()
    send_back(1)
    send_back(3, some=slice(None, CHIPS // 2))
    sums_x = many(ad_x.at[pl.ds(0, REPS - 1), pl.ds(0, 1)], s_send.at[1], s_recv.at[1])
    sums_x.wait_recv()
    ad_p[chip, pl.ds(0, 1), :] = jnp.sum(ad_x[:, pl.ds(0, 1), :], axis=0)
    for to in chips[1:]:
        pltpu.make_async_remote_copy(
            ad_p.at[chip, pl.ds(0, 1)], ad_p.at[chip, pl.ds(0, 1)], s_send.at[2], s_recv.at[2],
            device_id=(to * 2 + core, x), device_id_type=MESH,
        ).start()
    send_back(3, some=slice(CHIPS // 2, None))

    sums_plane = many(ad_p.at[pl.ds(0, CHIPS - 1), pl.ds(0, 1)], s_send.at[2], s_recv.at[2])
    sums_plane.wait_recv()
    total = jnp.sum(ad_p[:, pl.ds(0, 1), :], axis=0)
    line = lax.broadcasted_iota(jnp.int32, (nblk, 128), 0)
    lane = lax.broadcasted_iota(jnp.int32, (nblk, 128), 1)
    total = jnp.broadcast_to(total, (nblk, 128))
    area = width * width
    adam_mean = jnp.sum(jnp.where(lane == line, total, 0.0), axis=1, keepdims=True) / area
    prod_mean = jnp.sum(jnp.where(lane == line + nblk, total, 0.0), axis=1, keepdims=True) / area
    scale = jnp.sqrt(adam_mean) / jnp.sqrt(prod_mean + 1e-06)
    factor[...] = jnp.broadcast_to(scale, factor.shape)

    many(back.at[pl.ds(0, CHIPS * REPS - 1)], u_send.at[0], u_recv.at[0]).wait_recv()

    def collect(b, _):
        by = factor[pl.ds(b, 1), :]
        by = jnp.concatenate([by, by], axis=1)
        upd[b] = (wide(back[place[1, b]]) * by).astype(jnp.bfloat16)
        return 0

    lax.fori_loop(0, nblk, collect, 0, unroll=2)
    store_upd = pltpu.make_async_copy(upd, upd_hbm, sem_out.at[1])
    store_upd.start()

    many(xs.at[:, pl.ds(0, 6 * HALF)], x_send.at[0], x_recv.at[0, 0]).wait_send()
    many(f_out.at[:, pl.ds(0, CHIPS - 1)], f_send.at[0], f_recv.at[0]).wait_send()
    many(f_out, d_send.at[0], d_recv.at[0]).wait_send()
    many(ret, p_send.at[0], p_recv.at[0]).wait_send()
    for copy in (moments, sums_chip, sums_x, sums_plane):
        copy.wait_send()
    many(back.at[pl.ds(0, CHIPS * REPS - 1)], u_send.at[0], u_recv.at[0]).wait_send()
    store_nm.wait()
    store_upd.wait()


def one_kernel(grad, second_moment, left_factor, right_factor, block_owner, block_slot):
    nblk, rows, width = grad.shape
    slots = left_factor.shape[0]
    quarter = width // REPS
    bf, f32 = jnp.bfloat16, jnp.float32
    piece = (rows, quarter)
    part = (rows, width // CUTS)
    any_spec = pl.BlockSpec(memory_space=pl.ANY)
    vmem = pltpu.VMEM
    dma = pltpu.SemaphoreType.DMA
    return pl.pallas_call(
        step_kernel,
        out_shape=(
            jax.ShapeDtypeStruct((nblk, rows, quarter), bf),
            jax.ShapeDtypeStruct((nblk, rows, quarter), f32),
        ),
        in_specs=[pl.BlockSpec(memory_space=pltpu.SMEM)] * 2 + [any_spec] * 4,
        out_specs=(any_spec, any_spec),
        scratch_shapes=[
            vmem((nblk, rows, width), bf),
            vmem((nblk, rows, quarter), f32),
            vmem((slots, width, width), bf),
            vmem((slots, width, width), bf),
            vmem((CUTS, nblk) + part, bf),
            vmem((2, CUTS, HALF) + part, bf),
            vmem((2, CUTS, HALF) + part, bf),
            vmem((2, CUTS, HALF) + part, bf),
            vmem((2, CUTS, HALF) + part, bf),
            vmem((CUTS, PER_PLANE) + part, bf),
            vmem((CUTS, CHIPS) + part, bf),
            vmem((CUTS, CHIPS, 2) + part, bf),
            vmem((width, width), bf),
            vmem((2, width, quarter), f32),
        ]
        + [vmem((2, CHIPS, 2) + piece, bf)] * REPS
        + [
            vmem((REPS, CHIPS) + piece, bf),
            vmem((REPS * CHIPS,) + piece, bf),
            vmem((REPS, CUTS // REPS, PER_PLANE) + part, bf),
            vmem((nblk,) + piece, f32),
            vmem((nblk,) + piece, bf),
            vmem((16, 128), f32),
            vmem((REPS, 8, 128), f32),
            vmem((CHIPS, 8, 128), f32),
            vmem((nblk, 128), f32),
            vmem((8, 128), jnp.int32),
            pltpu.SMEM((8, 128), jnp.int32),
            vmem((8, 128), jnp.int32),
            pltpu.SMEM((8, 128), jnp.int32),
            dma((6,)),
            dma((2,)),
            dma((1,)),
            dma((CUTS, 2)),
            dma((1,)),
            dma((CUTS,)),
            dma((1,)),
            dma((CUTS,)),
            dma((1,)),
            dma((REPS,)),
        ]
        + [dma((1,))] * 4
        + [dma((3,))] * 2,
        compiler_params=pltpu.CompilerParams(
            collective_id=0, has_side_effects=True, vmem_limit_bytes=58 << 20
        ),
        cost_estimate=pl.CostEstimate(
            flops=4 * width**3, bytes_accessed=18 << 20, transcendentals=nblk * rows * quarter
        ),
        name="shampoo_step",
    )(block_owner, block_slot, grad, second_moment, left_factor, right_factor)


def crowded(block_owner, block_slot):
    bit = jnp.left_shift(jnp.int32(1), block_owner)
    other = jnp.left_shift(jnp.int32(1), block_owner ^ 1)
    third = jnp.sum(jnp.where(block_slot == 2, bit, 0))
    second = jnp.sum(jnp.where(block_slot == 1, other, 0))
    return (third & second) != 0


def ring_sum(value, axis):
    count = lax.axis_size(axis)
    step = 1
    while step < count:
        value = value + lax.ppermute(value, axis, [(i, i ^ step) for i in range(count)])
        step *= 2
    return value


def general(grad_partial, second_moment, left_factor, right_factor, block_owner, block_slot):
    slot_count = left_factor.shape[0]
    row_count = grad_partial.shape[2]
    full_width = grad_partial.shape[3]
    rep_count = lax.axis_size("rep")
    owner_count = lax.axis_size("fsdp")
    owner_index = lax.axis_index("fsdp")
    rep_index = lax.axis_index("rep")
    quarter = full_width // rep_count
    slot_range = jnp.arange(slot_count, dtype=jnp.int32)
    owner_range = jnp.arange(owner_count, dtype=jnp.int32)
    selector = (
        (block_slot[None, None, :] == slot_range[:, None, None])
        & (block_owner[None, None, :] == owner_range[None, :, None])
    ).astype(jnp.bfloat16)
    owned = (
        (block_slot[None, :] == slot_range[:, None]) & (block_owner[None, :] == owner_index)
    ).astype(jnp.float32)
    summed = ring_sum(grad_partial[0].astype(jnp.float32), "rep")
    column = lax.dynamic_slice_in_dim(summed, rep_index * quarter, quarter, 2)
    new_moment = 0.99 * second_moment + 0.01 * column * column
    adam = column / (jnp.sqrt(new_moment) + 1e-08)
    partial_squares = jnp.sum(adam * adam, axis=(1, 2))
    total_squares = ring_sum(ring_sum(partial_squares, "rep"), "fsdp")
    adam_rms = jnp.sqrt(total_squares / (full_width * full_width))
    slot_rms = jnp.sum(owned * adam_rms[None, :], axis=1)
    grad_bf = summed.astype(jnp.bfloat16)
    outbound = jnp.einsum(
        "kdn,nrc->kdrc", selector, grad_bf, preferred_element_type=jnp.float32
    ).astype(jnp.bfloat16)
    outbound = outbound.reshape(slot_count, owner_count * row_count, full_width)
    inbound = lax.all_to_all(outbound, "fsdp", split_axis=1, concat_axis=1, tiled=True)
    left_prod = jnp.einsum(
        "kij,kjc->kic", left_factor, inbound, preferred_element_type=jnp.float32
    ).astype(jnp.bfloat16)
    product = jnp.einsum(
        "kij,kjc->kic", left_prod, right_factor, preferred_element_type=jnp.float32
    )
    prod_mean = jnp.mean(product * product, axis=(1, 2))
    graft = slot_rms / jnp.sqrt(prod_mean + 1e-06)
    scaled = (product * graft[:, None, None]).astype(jnp.bfloat16)
    returned = lax.all_to_all(scaled, "fsdp", split_axis=1, concat_axis=1, tiled=True)
    returned = lax.dynamic_slice_in_dim(returned, rep_index * quarter, quarter, 2)
    returned = returned.reshape(slot_count, owner_count, row_count, quarter)
    update = jnp.einsum(
        "kdn,kdrc->nrc", selector, returned, preferred_element_type=jnp.float32
    ).astype(jnp.bfloat16)
    return (update, new_moment)


def per_device(grad_partial, second_moment, left_factor, right_factor, block_owner, block_slot):
    def direct(gp, sm, lf, rf, owner, slot):
        return one_kernel(gp[0], sm, lf, rf, owner, slot)

    return lax.cond(
        crowded(block_owner, block_slot), general, direct,
        grad_partial, second_moment, left_factor, right_factor, block_owner, block_slot,
    )


def solution(mesh):
    placed = (
        P("rep", None, "fsdp", None),
        P(None, "fsdp", "rep"),
        P("fsdp", None, None),
        P("fsdp", None, None),
        P(),
        P(),
    )
    return jax.shard_map(
        per_device,
        mesh=mesh,
        in_specs=placed,
        out_specs=(P(None, "fsdp", "rep"), P(None, "fsdp", "rep")),
        check_vma=False,
    )
```

```python
import functools

import jax
import jax.numpy as jnp
from jax import lax
from jax.experimental import pallas as pl
from jax.experimental.pallas import tpu as pltpu
from jax.sharding import PartitionSpec as P

MESH = pl.DeviceIdType.MESH
REPS = 4
CHIPS = 16
SIDE = 4
PER_PLANE = 8
HALF = PER_PLANE // 2
CUTS = 4


def step_kernel(
    owner, owner_slot, g_hbm, sm_hbm, l_hbm, r_hbm, upd_hbm, nm_hbm,
    grad, sm, left, right, xs, a_in, b_in, c_in, c_out, summed, f_out, g_in,
    lp, pb0, pb1, pb2, pb3, ret, back, mom_in, nm, upd,
    ad_1, ad_x, ad_p, factor, place_v, place, inverse_v, inverse,
    sem_in, sem_out, x_send, x_recv, f_send, f_recv, d_send, d_recv,
    p_send, p_recv, u_send, u_recv, m_send, m_recv, s_send, s_recv,
):
    pbs = (pb0, pb1, pb2, pb3)
    f = lax.axis_index("fsdp")
    x = lax.axis_index("rep")
    core = f % 2
    chip = f // 2
    cy = chip // SIDE
    cz = chip % SIDE
    sibling = f + 1 - 2 * core
    nblk, rows, width = grad.shape
    quarter = width // REPS
    cut = width // CUTS
    per_quarter = CUTS // REPS

    chips = [
        lax.rem(cy + i // SIDE, SIDE) * SIDE + lax.rem(cz + i % SIDE, SIDE)
        for i in (0, 10, 6, 9, 14, 11, 5, 15, 7, 13, 2, 8, 1, 4, 3, 12)
    ]
    reps = [lax.rem(x + i, REPS) for i in range(REPS)]

    loads = [
        pltpu.make_async_copy(src, dst, sem_in.at[i])
        for i, (src, dst) in enumerate(
            ((g_hbm, grad), (l_hbm, left), (r_hbm, right), (sm_hbm, sm))
        )
    ]
    for load in loads:
        load.start()

    barrier = pltpu.get_barrier_semaphore()

    for i in range(1, CHIPS * REPS):
        to = (chips[i // REPS] * 2 + core, reps[i % REPS])
        pl.semaphore_signal(barrier, inc=1, device_id=to, device_id_type=MESH)
    pl.semaphore_signal(barrier, inc=1, device_id=(sibling, x), device_id_type=MESH)

    lane = lax.broadcasted_iota(jnp.int32, place_v.shape, 1)
    line = lax.broadcasted_iota(jnp.int32, place_v.shape, 0)
    zero = jnp.zeros(place_v.shape, jnp.int32)
    owners, slots, before = zero, zero, zero
    for b in range(nblk):
        owners = jnp.where(lane == b, owner[b], owners)
        slots = jnp.where(lane == b, owner_slot[b], slots)
    for b in range(nblk):
        before = before + jnp.where(owners > owner[b], 1, 0)
    spot = before + slots
    plane_v = spot & (REPS - 1)
    sorted_v = plane_v * PER_PLANE + (spot >> 2)
    place_v[...] = jnp.where(line == 0, sorted_v, plane_v * CHIPS + (owners >> 1))
    to_scalar = pltpu.make_async_copy(place_v, place, sem_in.at[4])
    to_scalar.start()
    to_scalar.wait()
    order_v, dest_v = zero, zero
    slot = holder = mine = have = jnp.int32(0)
    for b in range(nblk):
        at, site = place[0, b], place[1, b]
        order_v = jnp.where(lane == at, b, order_v)
        dest_v = jnp.where(lane == site, at & (PER_PLANE - 1), dest_v)
        here = site == x * CHIPS + chip
        own = here & (owner[b] == f)
        holder = jnp.where(here, owner[b] & 1, holder)
        slot = jnp.where(own, owner_slot[b], slot)
        mine = jnp.where(own, b, mine)
        have = jnp.where(own, 1, have)
    inverse_v[...] = jnp.where(line == 0, order_v, dest_v)
    to_scalar = pltpu.make_async_copy(inverse_v, inverse, sem_in.at[5])
    to_scalar.start()
    to_scalar.wait()
    _, x_right, x_far, x_left = reps

    def many(ref, send, recv):
        return pltpu.make_async_remote_copy(
            ref, ref, send, recv, device_id=(sibling, x), device_id_type=MESH
        )

    def stage(k):
        def body(t, _):
            xs[k, t] = grad[inverse[0, t], :, k * cut : (k + 1) * cut]
            return 0

        lax.fori_loop(0, nblk, body, 0, unroll=4)

    def x_copy(k, n, src, dst, to):
        return pltpu.make_async_remote_copy(
            src, dst, x_send.at[0], x_recv.at[k, min(n // 2, 1)], device_id=(f, to), device_id_type=MESH
        )

    def x_copies(k):
        far, near_r, near_l = x_far * PER_PLANE, x_right * PER_PLANE, x_left * PER_PLANE
        return (
            x_copy(k, 0, xs.at[k, pl.ds(far, HALF)], a_in.at[0, k], x_right),
            x_copy(k, 1, xs.at[k, pl.ds(far + HALF, HALF)], a_in.at[1, k], x_left),
            x_copy(k, 2, xs.at[k, pl.ds(near_r + HALF, HALF)], b_in.at[0, k], x_right),
            x_copy(k, 3, xs.at[k, pl.ds(near_l, HALF)], b_in.at[1, k], x_left),
            x_copy(k, 4, c_out.at[0, k], c_in.at[0, k], x_right),
            x_copy(k, 5, c_out.at[1, k], c_in.at[1, k], x_left),
        )

    xc = [x_copies(k) for k in range(CUTS)]

    def first(k):
        xc[k][0].start()
        xc[k][1].start()

    def second(k):
        xc[k][2].start()
        xc[k][3].start()

    def wide(v):
        return v.astype(jnp.float32)

    def merge(k):
        many(xs.at[k, pl.ds(0, PER_PLANE)], x_send.at[0], x_recv.at[k, 0]).wait_recv()
        for side, at in ((0, x_right * PER_PLANE), (1, x_left * PER_PLANE + HALF)):

            def body(j, _):
                c_out[side, k, j] = (wide(xs[k, at + j]) + wide(a_in[side, k, j])).astype(jnp.bfloat16)
                return 0

            lax.fori_loop(0, HALF, body, 0, unroll=True)
            xc[k][4 + side].start()

    def finish(k):
        many(xs.at[k, pl.ds(0, 2 * PER_PLANE)], x_send.at[0], x_recv.at[k, 1]).wait_recv()
        for lo, from_l, from_r in ((0, c_in, b_in), (HALF, b_in, c_in)):

            def body(j, _):
                total = wide(xs[k, x * PER_PLANE + lo + j]) + wide(from_l[0, k, j]) + wide(from_r[1, k, j])
                summed[k, lo + j] = total.astype(jnp.bfloat16)
                return 0

            lax.fori_loop(0, HALF, body, 0, unroll=True)

    def forward(k):
        for to in chips[1:]:
            f_out[k, to] = summed[k, inverse[1, x * CHIPS + to]]
            pltpu.make_async_remote_copy(
                f_out.at[k, to], g_in.at[k, chip, core], f_send.at[0], f_recv.at[k],
                device_id=(to * 2 + core, x), device_id_type=MESH,
            ).start()
        g_in[k, chip, core] = summed[k, inverse[1, x * CHIPS + chip]]

    swaps = [
        pltpu.make_async_remote_copy(
            g_in.at[k, :, core], g_in.at[k, :, core], d_send.at[0], d_recv.at[k],
            device_id=(sibling, x), device_id_type=MESH,
        )
        for k in range(CUTS)
    ]

    def swap(k):
        many(f_out.at[k, pl.ds(0, CHIPS - 1)], f_send.at[0], f_recv.at[k]).wait_recv()
        swaps[k].start()

    def left_mul(m):
        parts = range(m * per_quarter, (m + 1) * per_quarter)
        for k in parts:
            swaps[k].wait_recv()

        block = jnp.concatenate([g_in[k].reshape(width, cut) for k in parts], axis=1)
        part = jnp.dot(left[slot], block, preferred_element_type=jnp.float32)
        lp[:, m * quarter : (m + 1) * quarter] = part.astype(jnp.bfloat16)

    loads[0].wait()
    stage(0)
    pl.semaphore_wait(barrier, CHIPS * REPS)
    first(0)
    second(0)
    for k in range(1, CUTS + 1):
        if k < CUTS:
            stage(k)
            first(k)
        merge(k - 1)
        if k < CUTS:
            second(k)
        if k == CUTS:
            swap(0)
        if k >= 2:
            finish(k - 2)
            forward(k - 2)
    swap(1)
    finish(CUTS - 1)
    forward(CUTS - 1)

    for i in range(1, REPS):
        to = reps[i]
        pltpu.make_async_remote_copy(
            summed.at[pl.ds(to * per_quarter, per_quarter)], mom_in.at[x], m_send.at[0], m_recv.at[0],
            device_id=(f, to), device_id_type=MESH,
        ).start()
    mom_in[x] = summed[pl.ds(x * per_quarter, per_quarter)]

    loads[1].wait()
    left_mul(0)
    left_mul(1)
    swap(2)
    left_mul(2)
    loads[2].wait()
    swap(3)
    left_mul(3)

    def right_mul(i, squares):
        cols = pl.ds(pl.multiple_of(reps[i] * quarter, quarter), quarter)
        part = jnp.dot(lp[...], right[slot, :, cols], preferred_element_type=jnp.float32)
        pbs[i][core] = part.astype(jnp.bfloat16).reshape(CHIPS, 2, rows, quarter)
        return squares + jnp.sum(part * part, axis=0, keepdims=True)

    trades = [
        pltpu.make_async_remote_copy(
            pb.at[core, :, 1 - core], pb.at[core, :, 1 - core], p_send.at[0], p_recv.at[i],
            device_id=(sibling, x), device_id_type=MESH,
        )
        for i, pb in enumerate(pbs)
    ]

    def send_back(*which, some=slice(None)):
        for i in which:
            if some.start is None:
                trades[i].wait_recv()
        for to in chips[some]:
            for i in which:
                if i == 0 and to is chips[0]:
                    back[x * CHIPS + chip] = pbs[i][holder, chip, core]
                    continue
                ret[i, to] = pbs[i][holder, to, core]
                pltpu.make_async_remote_copy(
                    ret.at[i, to], back.at[x * CHIPS + chip], u_send.at[0], u_recv.at[0],
                    device_id=(to * 2 + core, reps[i]), device_id_type=MESH,
                ).start()

    squares = jnp.zeros((1, quarter), jnp.float32)
    for i in (2, 0, 1, 3):
        squares = right_mul(i, squares)
        trades[i].start()
        if i == 0:
            send_back(2)
        if i == 1:
            send_back(0)

    loads[3].wait()
    moments = many(xs.at[0, pl.ds(0, (REPS - 1) * PER_PLANE)], m_send.at[0], m_recv.at[0])
    moments.wait_recv()

    at_lane = lax.broadcasted_iota(jnp.int32, (1, 128), 1)

    def moment(b, sums):
        t = place[0, b]
        sq = jnp.zeros((1, cut), jnp.float32)
        for h in range(per_quarter):
            s = wide(mom_in[t >> 3, h, t & (PER_PLANE - 1)])
            at = slice(h * cut, (h + 1) * cut)
            new = 0.99 * sm[b, :, at] + 0.01 * s * s
            nm[b, :, at] = new
            adam = s / (jnp.sqrt(new) + 1e-08)
            sq = sq + jnp.sum(adam * adam, axis=0, keepdims=True)
        return jnp.where(at_lane == b, jnp.sum(sq, axis=1, keepdims=True), sums)

    owned = (at_lane == nblk + mine) & (have == 1)
    own_sums = jnp.where(owned, jnp.sum(squares, axis=1, keepdims=True), 0.0)
    own_sums = lax.fori_loop(0, nblk, moment, own_sums, unroll=4)
    ad_1[pl.ds(0, 1), :] = own_sums
    sums_chip = pltpu.make_async_remote_copy(
        ad_1.at[pl.ds(0, 1)], ad_1.at[pl.ds(8, 1)], s_send.at[0], s_recv.at[0],
        device_id=(sibling, x), device_id_type=MESH,
    )
    sums_chip.start()
    store_nm = pltpu.make_async_copy(nm, nm_hbm, sem_out.at[0])
    store_nm.start()
    sums_chip.wait_recv()
    ad_x[x, pl.ds(0, 1), :] = own_sums + ad_1[pl.ds(8, 1), :]
    for i in range(1, REPS):
        pltpu.make_async_remote_copy(
            ad_x.at[x, pl.ds(0, 1)], ad_x.at[x, pl.ds(0, 1)], s_send.at[1], s_recv.at[1],
            device_id=(f, reps[i]), device_id_type=MESH,
        ).start()
    send_back(1)
    send_back(3, some=slice(None, CHIPS // 2))
    sums_x = many(ad_x.at[pl.ds(0, REPS - 1), pl.ds(0, 1)], s_send.at[1], s_recv.at[1])
    sums_x.wait_recv()
    ad_p[chip, pl.ds(0, 1), :] = jnp.sum(ad_x[:, pl.ds(0, 1), :], axis=0)
    for to in chips[1:]:
        pltpu.make_async_remote_copy(
            ad_p.at[chip, pl.ds(0, 1)], ad_p.at[chip, pl.ds(0, 1)], s_send.at[2], s_recv.at[2],
            device_id=(to * 2 + core, x), device_id_type=MESH,
        ).start()
    send_back(3, some=slice(CHIPS // 2, None))

    sums_plane = many(ad_p.at[pl.ds(0, CHIPS - 1), pl.ds(0, 1)], s_send.at[2], s_recv.at[2])
    sums_plane.wait_recv()
    total = jnp.sum(ad_p[:, pl.ds(0, 1), :], axis=0)
    line = lax.broadcasted_iota(jnp.int32, (nblk, 128), 0)
    lane = lax.broadcasted_iota(jnp.int32, (nblk, 128), 1)
    total = jnp.broadcast_to(total, (nblk, 128))
    area = width * width
    adam_mean = jnp.sum(jnp.where(lane == line, total, 0.0), axis=1, keepdims=True) / area
    prod_mean = jnp.sum(jnp.where(lane == line + nblk, total, 0.0), axis=1, keepdims=True) / area
    scale = jnp.sqrt(adam_mean) / jnp.sqrt(prod_mean + 1e-06)
    factor[...] = jnp.broadcast_to(scale, factor.shape)

    many(back.at[pl.ds(0, CHIPS * REPS - 1)], u_send.at[0], u_recv.at[0]).wait_recv()

    def collect(b, _):
        by = factor[pl.ds(b, 1), :]
        by = jnp.concatenate([by, by], axis=1)
        upd[b] = (wide(back[place[1, b]]) * by).astype(jnp.bfloat16)
        return 0

    lax.fori_loop(0, nblk, collect, 0, unroll=2)
    store_upd = pltpu.make_async_copy(upd, upd_hbm, sem_out.at[1])
    store_upd.start()

    many(xs.at[:, pl.ds(0, 6 * HALF)], x_send.at[0], x_recv.at[0, 0]).wait_send()
    many(f_out.at[:, pl.ds(0, CHIPS - 1)], f_send.at[0], f_recv.at[0]).wait_send()
    many(f_out, d_send.at[0], d_recv.at[0]).wait_send()
    many(ret, p_send.at[0], p_recv.at[0]).wait_send()
    for copy in (moments, sums_chip, sums_x, sums_plane):
        copy.wait_send()
    many(back.at[pl.ds(0, CHIPS * REPS - 1)], u_send.at[0], u_recv.at[0]).wait_send()
    store_nm.wait()
    store_upd.wait()


def one_kernel(grad, second_moment, left_factor, right_factor, block_owner, block_slot):
    nblk, rows, width = grad.shape
    slots = left_factor.shape[0]
    quarter = width // REPS
    bf, f32 = jnp.bfloat16, jnp.float32
    piece = (rows, quarter)
    part = (rows, width // CUTS)
    any_spec = pl.BlockSpec(memory_space=pl.ANY)
    vmem = pltpu.VMEM
    dma = pltpu.SemaphoreType.DMA
    return pl.pallas_call(
        step_kernel,
        out_shape=(
            jax.ShapeDtypeStruct((nblk, rows, quarter), bf),
            jax.ShapeDtypeStruct((nblk, rows, quarter), f32),
        ),
        in_specs=[pl.BlockSpec(memory_space=pltpu.SMEM)] * 2 + [any_spec] * 4,
        out_specs=(any_spec, any_spec),
        scratch_shapes=[
            vmem((nblk, rows, width), bf),
            vmem((nblk, rows, quarter), f32),
            vmem((slots, width, width), bf),
            vmem((slots, width, width), bf),
            vmem((CUTS, nblk) + part, bf),
            vmem((2, CUTS, HALF) + part, bf),
            vmem((2, CUTS, HALF) + part, bf),
            vmem((2, CUTS, HALF) + part, bf),
            vmem((2, CUTS, HALF) + part, bf),
            vmem((CUTS, PER_PLANE) + part, bf),
            vmem((CUTS, CHIPS) + part, bf),
            vmem((CUTS, CHIPS, 2) + part, bf),
            vmem((width, width), bf),
        ]
        + [vmem((2, CHIPS, 2) + piece, bf)] * REPS
        + [
            vmem((REPS, CHIPS) + piece, bf),
            vmem((REPS * CHIPS,) + piece, bf),
            vmem((REPS, CUTS // REPS, PER_PLANE) + part, bf),
            vmem((nblk,) + piece, f32),
            vmem((nblk,) + piece, bf),
            vmem((16, 128), f32),
            vmem((REPS, 8, 128), f32),
            vmem((CHIPS, 8, 128), f32),
            vmem((nblk, 128), f32),
            vmem((8, 128), jnp.int32),
            pltpu.SMEM((8, 128), jnp.int32),
            vmem((8, 128), jnp.int32),
            pltpu.SMEM((8, 128), jnp.int32),
            dma((6,)),
            dma((2,)),
            dma((1,)),
            dma((CUTS, 2)),
            dma((1,)),
            dma((CUTS,)),
            dma((1,)),
            dma((CUTS,)),
            dma((1,)),
            dma((REPS,)),
        ]
        + [dma((1,))] * 4
        + [dma((3,))] * 2,
        compiler_params=pltpu.CompilerParams(
            collective_id=0, has_side_effects=True, vmem_limit_bytes=58 << 20
        ),
        cost_estimate=pl.CostEstimate(
            flops=4 * width**3, bytes_accessed=18 << 20, transcendentals=nblk * rows * quarter
        ),
        name="shampoo_step",
    )(block_owner, block_slot, grad, second_moment, left_factor, right_factor)


def crowded(block_owner, block_slot):
    bit = jnp.left_shift(jnp.int32(1), block_owner)
    other = jnp.left_shift(jnp.int32(1), block_owner ^ 1)
    third = jnp.sum(jnp.where(block_slot == 2, bit, 0))
    second = jnp.sum(jnp.where(block_slot == 1, other, 0))
    return (third & second) != 0


def ring_sum(value, axis):
    count = lax.axis_size(axis)
    step = 1
    while step < count:
        value = value + lax.ppermute(value, axis, [(i, i ^ step) for i in range(count)])
        step *= 2
    return value


def general(grad_partial, second_moment, left_factor, right_factor, block_owner, block_slot):
    slot_count = left_factor.shape[0]
    row_count = grad_partial.shape[2]
    full_width = grad_partial.shape[3]
    rep_count = lax.axis_size("rep")
    owner_count = lax.axis_size("fsdp")
    owner_index = lax.axis_index("fsdp")
    rep_index = lax.axis_index("rep")
    quarter = full_width // rep_count
    slot_range = jnp.arange(slot_count, dtype=jnp.int32)
    owner_range = jnp.arange(owner_count, dtype=jnp.int32)
    selector = (
        (block_slot[None, None, :] == slot_range[:, None, None])
        & (block_owner[None, None, :] == owner_range[None, :, None])
    ).astype(jnp.bfloat16)
    owned = (
        (block_slot[None, :] == slot_range[:, None]) & (block_owner[None, :] == owner_index)
    ).astype(jnp.float32)
    summed = ring_sum(grad_partial[0].astype(jnp.float32), "rep")
    column = lax.dynamic_slice_in_dim(summed, rep_index * quarter, quarter, 2)
    new_moment = 0.99 * second_moment + 0.01 * column * column
    adam = column / (jnp.sqrt(new_moment) + 1e-08)
    partial_squares = jnp.sum(adam * adam, axis=(1, 2))
    total_squares = ring_sum(ring_sum(partial_squares, "rep"), "fsdp")
    adam_rms = jnp.sqrt(total_squares / (full_width * full_width))
    slot_rms = jnp.sum(owned * adam_rms[None, :], axis=1)
    grad_bf = summed.astype(jnp.bfloat16)
    outbound = jnp.einsum(
        "kdn,nrc->kdrc", selector, grad_bf, preferred_element_type=jnp.float32
    ).astype(jnp.bfloat16)
    outbound = outbound.reshape(slot_count, owner_count * row_count, full_width)
    inbound = lax.all_to_all(outbound, "fsdp", split_axis=1, concat_axis=1, tiled=True)
    left_prod = jnp.einsum(
        "kij,kjc->kic", left_factor, inbound, preferred_element_type=jnp.float32
    ).astype(jnp.bfloat16)
    product = jnp.einsum(
        "kij,kjc->kic", left_prod, right_factor, preferred_element_type=jnp.float32
    )
    prod_mean = jnp.mean(product * product, axis=(1, 2))
    graft = slot_rms / jnp.sqrt(prod_mean + 1e-06)
    scaled = (product * graft[:, None, None]).astype(jnp.bfloat16)
    returned = lax.all_to_all(scaled, "fsdp", split_axis=1, concat_axis=1, tiled=True)
    returned = lax.dynamic_slice_in_dim(returned, rep_index * quarter, quarter, 2)
    returned = returned.reshape(slot_count, owner_count, row_count, quarter)
    update = jnp.einsum(
        "kdn,kdrc->nrc", selector, returned, preferred_element_type=jnp.float32
    ).astype(jnp.bfloat16)
    return (update, new_moment)


def per_device(grad_partial, second_moment, left_factor, right_factor, block_owner, block_slot):
    def direct(gp, sm, lf, rf, owner, slot):
        return one_kernel(gp[0], sm, lf, rf, owner, slot)

    return lax.cond(
        crowded(block_owner, block_slot), general, direct,
        grad_partial, second_moment, left_factor, right_factor, block_owner, block_slot,
    )


def solution(mesh):
    placed = (
        P("rep", None, "fsdp", None),
        P(None, "fsdp", "rep"),
        P("fsdp", None, None),
        P("fsdp", None, None),
        P(),
        P(),
    )
    return jax.shard_map(
        per_device,
        mesh=mesh,
        in_specs=placed,
        out_specs=(P(None, "fsdp", "rep"), P(None, "fsdp", "rep")),
        check_vma=False,
    )
```
